512 devices in a mesh: lon: 32 (over z_hi, y, x), lat: 16 (over z_lo, core).
Axes of the slice: x: 4, y: 4, z: 16 (z_hi: 2, z_lo: 8; z = z_hi * 8 + z_lo), core: 2. Of those that a mesh axis runs over, the one named last changes fastest.
Arguments:
- block_input: bfloat16 [2, 192, 384, 512], P(None, 'lat', 'lon')
- cotangent: bfloat16 [2, 192, 384, 512], P(None, 'lat', 'lon'), may hold values from -6 to 6
- norm_gain: float32 [512], replicated, may hold values from 0.1 to 1.9
- w_qkv: bfloat16 [512, 1536], replicated
- w_out: bfloat16 [512, 512], replicated, may hold values from -0.25 to 0.25
Outputs:
- input_grad: bfloat16 [2, 192, 384, 512], P(None, 'lat', 'lon')
- qkv_grad: float32 [512, 1536], P('lon')
- out_grad: float32 [512, 512], P('lon')
- gain_grad: float32 [512], replicated
The draws below stay inside these ranges and needn't reach their ends.
All inputs are finite; a program needn't handle non-finite values.
Results may differ from the reference program's by a relative error of at most 0.035.
The reference program's roundings to bfloat16 on the way count: a program that leaves them out, or rounds other values in their place, can miss the bound.
Values may be sent and summed in bfloat16 or wider, within the bound.
No kernel may reach another device: no remote copies, remote signals or barrier semaphores. Data moves between devices by JAX's collectives and lax.ppermute only.
A program may use at most 64 MiB of HBM per device.

```python
import math
import jax
import jax.numpy as jnp
from jax import lax

D = 512
HEADS = 16
LEV = 2
WLAT = 6
WLON = 12
NLAT = 192
NLON = 384


def draw_block_input(key, part):
    key = jax.random.fold_in(key, 11)
    shape = (LEV, NLAT, NLON, D)
    return jax.random.normal(key, shape, jnp.float32).astype(jnp.bfloat16)


def draw_w_qkv(key, part):
    key = jax.random.fold_in(key, 12)
    base = jax.random.normal(key, (D, 3 * D), jnp.float32) * D ** (-0.5)
    return base.astype(jnp.bfloat16)


def steps_of(stream_key, dims, shards, low, high):
    factor_of = 1.0
    for position, parts in shards:
        heights = jax.random.uniform(jax.random.fold_in(jax.random.fold_in(stream_key, 6), position), (parts,), jnp.float32, low / len(shards), high / len(shards))
        factor_of = factor_of * jnp.repeat(jnp.exp(heights), dims[position] // parts).reshape((-1,) + (1,) * (len(dims) - 1 - position))
    return factor_of


def scatter_about(key, shape, width, most, shards=(), kind=jnp.bfloat16):
    gain = steps_of(key, shape, shards, -0.22, 0.18) if shards else 1.0
    array = jax.random.normal(key, shape, jnp.float32) * width * gain
    return jnp.minimum(jnp.maximum(array, -most), most).astype(kind)


def setup_inputs(seed: int = 0) -> dict:
    splits = jax.random.split(jax.random.key(seed), 6)
    return {
        "block_input": draw_block_input(jax.random.fold_in(splits[5], 71), 0),
        "cotangent": scatter_about(splits[1], (LEV, NLAT, NLON, D), 1.0, 6.0, ((1, 16), (2, 32))),
        "norm_gain": jnp.clip(1.0 + 0.18 * jax.random.normal(splits[2], (D,), jnp.float32), 0.1, 1.9),
        "w_qkv": draw_w_qkv(jax.random.fold_in(splits[5], 71), 0),
        "w_out": scatter_about(splits[4], (D, D), D ** -0.5, 0.25),
    }


def layer_norm(inputs):
    values = inputs.astype(jnp.float32)
    centred = values - lax.optimization_barrier(jnp.mean(values, axis=-1, keepdims=True))
    inverse = lax.rsqrt(lax.optimization_barrier(jnp.mean(centred * centred, axis=-1, keepdims=True)) + 1e-05)
    return (centred * inverse, inverse)

def widen(values):
    return lax.optimization_barrier(values).astype(jnp.float32)

def reference(block_input, cotangent, norm_gain, w_qkv, w_out):
    half_lat = WLAT // 2
    half_lon = WLON // 2
    levels = block_input.shape[0]
    lat_all = block_input.shape[1]
    lon_all = block_input.shape[2]
    feature = block_input.shape[3]
    head_dim = feature // HEADS
    score_scale = 1.0 / math.sqrt(head_dim)
    band_count = lat_all // WLAT
    cycle_count = lon_all // WLON
    window_len = levels * WLAT * WLON

    def to_windows(field):
        shaped = field.reshape(levels, band_count, WLAT, cycle_count, WLON, feature)
        return shaped.transpose(1, 3, 0, 2, 4, 5).reshape(-1, window_len, feature)

    def label_windows(grid):
        shaped = grid.reshape(band_count, WLAT, cycle_count, WLON).transpose(0, 2, 1, 3)
        shaped = jnp.broadcast_to(shaped[:, :, None], (band_count, cycle_count, levels, WLAT, WLON))
        return shaped.reshape(-1, window_len)
    rolled_input = jnp.roll(block_input, (-half_lat, -half_lon), axis=(1, 2))
    rolled_grad = jnp.roll(cotangent, (-half_lat, -half_lon), axis=(1, 2))
    input_win = to_windows(rolled_input)
    grad_win = to_windows(rolled_grad)
    edge_rows = (jnp.arange(lat_all, dtype=jnp.int32) >= lat_all - half_lat).astype(jnp.int32)
    edge_grid = jnp.broadcast_to(edge_rows[:, None], (lat_all, lon_all))
    edge_win = label_windows(edge_grid)

    def window_step(totals, inputs):
        x_win, dy_win, edge_flag = inputs
        normed, inverse = layer_norm(x_win)
        hidden = (normed * norm_gain).astype(jnp.bfloat16)
        qkv = jnp.dot(hidden, w_qkv, preferred_element_type=jnp.float32).astype(jnp.bfloat16)
        d_attn = jnp.dot(dy_win, w_out.T, preferred_element_type=jnp.float32).astype(jnp.bfloat16)
        split = widen(qkv).reshape(window_len, 3, HEADS, head_dim)
        queries = split[:, 0]
        keys_win = split[:, 1]
        values_win = split[:, 2]
        grad_heads = widen(d_attn).reshape(window_len, HEADS, head_dim)
        scores = jnp.einsum('qhd,khd->hqk', queries, keys_win) * score_scale
        allowed = edge_flag[:, None] == edge_flag[None, :]
        row_max = lax.optimization_barrier(jnp.max(jnp.where(allowed, scores, -jnp.inf), axis=-1, keepdims=True))
        weights_raw = jnp.where(allowed, jnp.exp(scores - row_max), 0.0)
        prob_full = weights_raw / lax.optimization_barrier(jnp.sum(weights_raw, axis=-1, keepdims=True))
        prob_cast = widen(prob_full.astype(jnp.bfloat16))
        attended = jnp.einsum('hqk,khd->qhd', prob_cast, values_win).reshape(window_len, feature).astype(jnp.bfloat16)
        dprob = jnp.einsum('qhd,khd->hqk', grad_heads, values_win)
        row_delta = lax.optimization_barrier(jnp.sum(prob_full * dprob, axis=-1, keepdims=True))
        dscore = widen((prob_full * (dprob - row_delta) * score_scale).astype(jnp.bfloat16))
        dquery = jnp.einsum('hqk,khd->qhd', dscore, keys_win)
        dkey = jnp.einsum('hqk,qhd->khd', dscore, queries)
        dvalue = jnp.einsum('hqk,qhd->khd', prob_cast, grad_heads)
        dslab = jnp.stack([dquery, dkey, dvalue], axis=1).reshape(window_len, 3 * feature).astype(jnp.bfloat16)
        dhidden = jnp.dot(dslab, w_qkv.T, preferred_element_type=jnp.float32)
        gain_term = lax.optimization_barrier(jnp.sum(dhidden * normed, axis=0))
        dnorm = dhidden * norm_gain
        drolled = dy_win.astype(jnp.float32) + inverse * (dnorm - lax.optimization_barrier(jnp.mean(dnorm, axis=-1, keepdims=True)) - normed * lax.optimization_barrier(jnp.mean(dnorm * normed, axis=-1, keepdims=True)))
        qkv_total = totals[0] + jnp.dot(hidden.T, dslab, preferred_element_type=jnp.float32)
        out_total = totals[1] + jnp.dot(attended.T, dy_win, preferred_element_type=jnp.float32)
        gain_total = totals[2] + gain_term
        return ((qkv_total, out_total, gain_total), drolled.astype(jnp.bfloat16))
    start = (jnp.zeros((feature, 3 * feature), jnp.float32), jnp.zeros((feature, feature), jnp.float32), jnp.zeros((feature,), jnp.float32))
    totals, drolled_win = lax.scan(window_step, start, (input_win, grad_win, edge_win))
    grid = drolled_win.reshape(band_count, cycle_count, levels, WLAT, WLON, feature)
    grid = grid.transpose(2, 0, 3, 1, 4, 5).reshape(levels, lat_all, lon_all, feature)
    input_grad = jnp.roll(grid, (half_lat, half_lon), axis=(1, 2))
    return (input_grad, totals[0], totals[1], totals[2])
```

```python
import functools
import math

import jax
import jax.numpy as jnp
from jax import lax
from jax.experimental import pallas as pl
from jax.experimental.pallas import tpu as pltpu
from jax.sharding import Mesh, PartitionSpec as P

HEADS = 16
HEAD_DIM = 32
WLAT = 6
WLON = 12
WINDOW = 144
TOKENS = 288
BLOCK = 36
GROUP = 4
BF16 = jnp.bfloat16
F32 = jnp.float32
LON = ("zh", "y", "x")
LAT = ("zl", "c")
ALL = LON + LAT
MIDS = ((1, 1), (2, 1), (1, 2), (2, 2))


def nn(a, b):
    return lax.dot_general(a, b, (((1,), (0,)), ((), ())), preferred_element_type=F32)


def nt(a, b):
    return lax.dot_general(a, b, (((1,), (1,)), ((), ())), preferred_element_type=F32)


def tn(a, b):
    return lax.dot_general(a, b, (((0,), (0,)), ((), ())), preferred_element_type=F32)


def attention_group(window, group, last, qkv, d_attn, attended, dqkv):
    feature = HEADS * HEAD_DIM
    width = GROUP * HEAD_DIM
    rows = pl.ds(pl.multiple_of(window * WINDOW, 16), WINDOW)
    at = group * width

    def columns(offset):
        return pl.ds(pl.multiple_of(at + offset, 128), width)

    queries = qkv[rows, columns(0)]
    keys = qkv[rows, columns(feature)]
    values = qkv[rows, columns(2 * feature)]
    grads = d_attn[rows, columns(0)]
    scale = 1.0 / math.sqrt(HEAD_DIM)
    lane_head = lax.broadcasted_iota(jnp.int32, (1, width), 1) // HEAD_DIM
    half = WINDOW // 2
    key_late = lax.broadcasted_iota(jnp.int32, (WINDOW, WINDOW), 0) >= half
    query_late = lax.broadcasted_iota(jnp.int32, (WINDOW, WINDOW), 1) >= half
    masked = jnp.logical_and(last == 1, window == 1)
    allowed = jnp.logical_or(key_late == query_late, jnp.logical_not(masked))

    dkey = jnp.zeros((WINDOW, width), F32)
    dvalue = jnp.zeros((WINDOW, width), F32)
    prob_parts, dscore_parts, key_parts, value_parts = [], [], [], []
    for head in range(GROUP):
        own = (lane_head == head).astype(BF16)
        keys_h = keys * own
        values_h = values * own
        scores = nt(keys_h, queries) * scale
        scores = jnp.where(allowed, scores, -jnp.inf)
        weights = jnp.exp(scores - jnp.max(scores, axis=0, keepdims=True))
        prob = weights * (1.0 / jnp.sum(weights, axis=0, keepdims=True))
        dprob = nt(values_h, grads)
        delta = jnp.sum(prob * dprob, axis=0, keepdims=True)
        dscore = (prob * (dprob - delta) * scale).astype(BF16)
        prob = prob.astype(BF16)
        dkey = dkey + nn(dscore, queries * own)
        dvalue = dvalue + nn(prob, grads * own)
        prob_parts.append(prob)
        dscore_parts.append(dscore)
        key_parts.append(keys_h)
        value_parts.append(values_h)
    prob_all = jnp.concatenate(prob_parts, axis=0)
    dscore_all = jnp.concatenate(dscore_parts, axis=0)
    attended[rows, columns(0)] = tn(prob_all, jnp.concatenate(value_parts, axis=0)).astype(BF16)
    dqkv[rows, columns(0)] = tn(dscore_all, jnp.concatenate(key_parts, axis=0)).astype(BF16)
    dqkv[rows, columns(feature)] = dkey.astype(BF16)
    dqkv[rows, columns(2 * feature)] = dvalue.astype(BF16)


def block_kernel(
    place, x_ref, dy_ref, gain_ref, w_qkv_ref, w_out_ref,
    drolled_ref, keep_ref, send_ref,
    normed_ref, hidden_ref, qkv_ref, d_attn_ref, attended_ref, dqkv_ref, total_ref,
):
    last = place[0]
    core = place[1]
    feature = HEADS * HEAD_DIM
    values = x_ref[...].astype(F32)
    centred = values - jnp.mean(values, axis=-1, keepdims=True)
    inverse = lax.rsqrt(jnp.mean(centred * centred, axis=-1, keepdims=True) + 1e-05)
    normed_ref[...] = centred * inverse
    hidden_ref[...] = (normed_ref[...] * gain_ref[...]).astype(BF16)
    qkv_ref[...] = nn(hidden_ref[...], w_qkv_ref[...]).astype(BF16)
    d_attn_ref[...] = nt(dy_ref[...], w_out_ref[...]).astype(BF16)

    groups = HEADS // GROUP

    @pl.loop(0, (TOKENS // WINDOW) * groups)
    def _(step):
        attention_group(
            step // groups, step % groups, last, qkv_ref, d_attn_ref, attended_ref, dqkv_ref
        )

    total_ref[:, 0 : 3 * feature] = tn(hidden_ref[...], dqkv_ref[...]).astype(BF16)
    total_ref[:, 3 * feature : 4 * feature] = tn(attended_ref[...], dy_ref[...]).astype(BF16)
    dhidden = nt(dqkv_ref[...], w_qkv_ref[...])
    normed = normed_ref[...]
    gain_local = jnp.sum(dhidden * normed, axis=0, keepdims=True)
    dnorm = dhidden * gain_ref[...]
    drolled = dy_ref[...].astype(F32) + inverse * (
        dnorm
        - jnp.mean(dnorm, axis=-1, keepdims=True)
        - normed * jnp.mean(dnorm * normed, axis=-1, keepdims=True)
    )
    drolled_ref[...] = drolled.astype(BF16)

    coarse = gain_local.astype(BF16)
    fine = (gain_local - coarse.astype(F32)).astype(BF16)
    gain_rows = [coarse[:, 128 * j : 128 * (j + 1)] for j in range(4)]
    gain_rows += [fine[:, 128 * j : 128 * (j + 1)] for j in range(4)]
    gain_tile = jnp.concatenate(
        [row.astype(F32) for row in gain_rows] + [jnp.zeros((8, 128), F32)], axis=0
    ).astype(BF16)

    @pl.loop(0, 16)
    def _(chunk):
        for half, out in ((core, keep_ref), (1 - core, send_ref)):
            start = pl.multiple_of(half * 256 + chunk * 16, 16)
            rows = total_ref[pl.ds(start, 16), :]
            for j in range(16):
                out[chunk, j] = rows[:, 128 * j : 128 * (j + 1)]
            out[chunk, 16] = gain_tile


def block(place, tokens, grads, norm_gain, w_qkv, w_out):
    feature = HEADS * HEAD_DIM
    vmem = pl.BlockSpec(memory_space=pltpu.VMEM)
    chunks = jax.ShapeDtypeStruct((16, 17, 16, 128), BF16)
    return pl.pallas_call(
        block_kernel,
        out_shape=(jax.ShapeDtypeStruct((TOKENS, feature), BF16), chunks, chunks),
        in_specs=[pl.BlockSpec(memory_space=pltpu.SMEM)] + [vmem] * 5,
        out_specs=(vmem, vmem, vmem),
        scratch_shapes=[
            pltpu.VMEM((TOKENS, feature), F32),
            pltpu.VMEM((TOKENS, feature), BF16),
            pltpu.VMEM((TOKENS, 3 * feature), BF16),
            pltpu.VMEM((TOKENS, feature), BF16),
            pltpu.VMEM((TOKENS, feature), BF16),
            pltpu.VMEM((TOKENS, 3 * feature), BF16),
            pltpu.VMEM((feature, 4 * feature), BF16),
        ],
        compiler_params=pltpu.CompilerParams(vmem_limit_bytes=40 * 1024 * 1024),
        cost_estimate=pl.CostEstimate(
            flops=2_000_000_000, bytes_accessed=6_000_000, transcendentals=700_000
        ),
        name="window_block",
    )(place, tokens, grads, norm_gain, w_qkv, w_out)


def index(zh, y, x, zl, c):
    return (((zh * 4 + y) * 4 + x) * 8 + zl) * 2 + c


def fetch_lon(pieces, diagonal):
    inside = [(i + 1, i) for i in range(32) if i % 16 != 15]
    normal = lax.ppermute(pieces, LON, inside)
    normal_diagonal = lax.ppermute(
        diagonal, ALL,
        [((i + 1) * 16 + (j + 1) % 16, i * 16 + j) for i in range(32) if i % 16 != 15 for j in range(16)],
    )
    crossing = []
    for k, (y, x) in enumerate(MIDS):
        shift = 1 if k == 3 else 0
        out, across = [], []
        for zh in range(2):
            for lat in range(16):
                zl, c = lat // 2, lat % 2
                source = (lat + shift) % 16
                middle = index(zh, y, x, zl, c)
                out.append((index(zh, 0, 0, source // 2, source % 2), middle))
                across.append((middle, index(1 - zh, 3, 3, zl, c)))
        part = diagonal if k == 3 else pieces[k]
        crossing.append(lax.ppermute(lax.ppermute(part, ALL, out), ALL, across))
    east = lax.axis_index(LON) % 16 == 15
    arrived = [jnp.where(east, crossing[k], normal[k]) for k in range(3)]
    return arrived + [jnp.where(east, crossing[3], normal_diagonal)]


def per_device(block_input, cotangent, norm_gain, w_qkv, w_out):
    half_lat, half_lon = WLAT // 2, WLON // 2
    levels, lat_rows, lon_cols, feature = block_input.shape
    stacked = jnp.stack([block_input, cotangent])

    def part(row, col):
        return stacked[:, :, row : row + half_lat, col : col + half_lon].reshape(2, BLOCK, feature)

    west = jnp.stack([part(row, 0) for row in (3, 6, 9)])
    diagonal = part(0, 0)
    lat_block = lax.ppermute(part(0, half_lon), LAT, [((i + 1) % 16, i) for i in range(16)])
    p0, p1, p2, corner = fetch_lon(west, diagonal)
    own = [part(row, half_lon) for row in (3, 6, 9)]
    tokens = jnp.concatenate([own[0], own[1], p0, p1, own[2], p2, lat_block, corner], axis=1)
    last = (lax.axis_index(LAT) == lax.axis_size("zl") * lax.axis_size("c") - 1).astype(jnp.int32)
    place = jnp.stack([last, lax.axis_index("c").astype(jnp.int32)])
    drolled, keep, send = block(
        place, tokens[0], tokens[1], norm_gain.reshape(1, feature), w_qkv, w_out
    )

    parts = drolled.reshape(8, BLOCK, feature)
    back_lon = lax.ppermute(
        jnp.stack([parts[2], parts[3], parts[5]]), LON, [(i, (i + 1) % 32) for i in range(32)]
    )
    back_lat = lax.ppermute(parts[6], LAT, [(i, (i + 1) % 16) for i in range(16)])
    back_corner = lax.ppermute(
        parts[7], ALL,
        [(i * 16 + j, ((i + 1) % 32) * 16 + (j + 1) % 16) for i in range(32) for j in range(16)],
    )

    def grid(piece):
        return piece.reshape(levels, half_lat, half_lon, feature)

    top = jnp.concatenate([grid(back_corner), grid(back_lat)], axis=2)
    rest = [
        jnp.concatenate([grid(back_lon[k]), grid(parts[own_at])], axis=2)
        for k, own_at in enumerate((0, 1, 4))
    ]
    input_grad = jnp.concatenate([top] + rest, axis=1)

    other = lax.ppermute(send, "c", [(0, 1), (1, 0)])
    pair = (keep.astype(F32) + other.astype(F32)).astype(BF16)
    plane = lax.all_to_all(pair, ("y", "x"), 0, 0, tiled=True)
    plane = jnp.sum(plane.astype(F32), axis=0)
    gain_part = jnp.broadcast_to(plane[16].astype(BF16), (16, 16, 128))
    column = lax.all_to_all(
        jnp.stack([plane[:16].astype(BF16), gain_part], axis=1), ("zh", "zl"), 0, 0, tiled=True
    )
    column = jnp.sum(column.astype(F32), axis=0)
    gain_rows = column[1]
    gain_grad = (gain_rows[0:4] + gain_rows[4:8]).reshape(feature)
    final = column[0].astype(BF16)
    fan = jnp.broadcast_to(final, (32, 16, 128))
    gathered = lax.all_to_all(fan, ("zh", "zl", "c"), 0, 0, tiled=True)
    gathered = gathered.reshape(16, 2, 16, 128)
    mine = lax.dynamic_index_in_dim(gathered, lax.axis_index("zh"), axis=1, keepdims=False)
    weights = mine.transpose(1, 0, 2).reshape(16, 4 * feature).astype(F32)
    return input_grad, weights[:, : 3 * feature], weights[:, 3 * feature :], gain_grad


def solution(mesh):
    fine = Mesh(mesh.devices.reshape(2, 4, 4, 8, 2), ALL)
    grid_spec = P(None, LAT, LON, None)
    return jax.shard_map(
        per_device,
        mesh=fine,
        in_specs=(grid_spec, grid_spec, P(), P(), P()),
        out_specs=(grid_spec, P(LON, None), P(LON, None), P()),
        check_vma=False,
    )
```

```python
import functools
import math

import jax
import jax.numpy as jnp
from jax import lax
from jax.experimental import pallas as pl
from jax.experimental.pallas import tpu as pltpu
from jax.sharding import Mesh, PartitionSpec as P

HEADS = 16
HEAD_DIM = 32
WLAT = 6
WLON = 12
WINDOW = 144
TOKENS = 288
BLOCK = 36
GROUP = 4
BF16 = jnp.bfloat16
F32 = jnp.float32
LON = ("zh", "y", "x")
LAT = ("zl", "c")
ALL = LON + LAT
MIDS = ((0, 3), (3, 0), (3, 1), (1, 3))


def nn(a, b):
    return lax.dot_general(a, b, (((1,), (0,)), ((), ())), preferred_element_type=F32)


def nt(a, b):
    return lax.dot_general(a, b, (((1,), (1,)), ((), ())), preferred_element_type=F32)


def tn(a, b):
    return lax.dot_general(a, b, (((0,), (0,)), ((), ())), preferred_element_type=F32)


def attention_group(window, group, last, qkv, d_attn, attended, dqkv):
    feature = HEADS * HEAD_DIM
    width = GROUP * HEAD_DIM
    rows = pl.ds(pl.multiple_of(window * WINDOW, 16), WINDOW)
    at = group * width

    def columns(offset):
        return pl.ds(pl.multiple_of(at + offset, 128), width)

    queries = qkv[rows, columns(0)]
    keys = qkv[rows, columns(feature)]
    values = qkv[rows, columns(2 * feature)]
    grads = d_attn[rows, columns(0)]
    scale = 1.0 / math.sqrt(HEAD_DIM)
    lane_head = lax.broadcasted_iota(jnp.int32, (1, width), 1) // HEAD_DIM
    half = WINDOW // 2
    key_late = lax.broadcasted_iota(jnp.int32, (WINDOW, WINDOW), 0) >= half
    query_late = lax.broadcasted_iota(jnp.int32, (WINDOW, WINDOW), 1) >= half
    masked = jnp.logical_and(last == 1, window == 1)
    allowed = jnp.logical_or(key_late == query_late, jnp.logical_not(masked))

    dkey = jnp.zeros((WINDOW, width), F32)
    dvalue = jnp.zeros((WINDOW, width), F32)
    prob_parts, dscore_parts, key_parts, value_parts = [], [], [], []
    for head in range(GROUP):
        own = (lane_head == head).astype(BF16)
        keys_h = keys * own
        values_h = values * own
        scores = nt(keys_h, queries) * scale
        scores = jnp.where(allowed, scores, -jnp.inf)
        weights = jnp.exp(scores - jnp.max(scores, axis=0, keepdims=True))
        prob = weights * (1.0 / jnp.sum(weights, axis=0, keepdims=True))
        dprob = nt(values_h, grads)
        delta = jnp.sum(prob * dprob, axis=0, keepdims=True)
        dscore = (prob * (dprob - delta) * scale).astype(BF16)
        prob = prob.astype(BF16)
        dkey = dkey + nn(dscore, queries * own)
        dvalue = dvalue + nn(prob, grads * own)
        prob_parts.append(prob)
        dscore_parts.append(dscore)
        key_parts.append(keys_h)
        value_parts.append(values_h)
    prob_all = jnp.concatenate(prob_parts, axis=0)
    dscore_all = jnp.concatenate(dscore_parts, axis=0)
    attended[rows, columns(0)] = tn(prob_all, jnp.concatenate(value_parts, axis=0)).astype(BF16)
    dqkv[rows, columns(0)] = tn(dscore_all, jnp.concatenate(key_parts, axis=0)).astype(BF16)
    dqkv[rows, columns(feature)] = dkey.astype(BF16)
    dqkv[rows, columns(2 * feature)] = dvalue.astype(BF16)


def block_kernel(
    place, x_ref, dy_ref, gain_ref, w_qkv_ref, w_out_ref,
    drolled_ref, back_ref, hidden_ref, dqkv_ref, attended_ref, gain_tile_ref,
    normed_ref, qkv_ref, d_attn_ref,
):
    last = place[0]
    values = x_ref[...].astype(F32)
    centred = values - jnp.mean(values, axis=-1, keepdims=True)
    inverse = lax.rsqrt(jnp.mean(centred * centred, axis=-1, keepdims=True) + 1e-05)
    normed_ref[...] = centred * inverse
    hidden_ref[...] = (normed_ref[...] * gain_ref[...]).astype(BF16)
    qkv_ref[...] = nn(hidden_ref[...], w_qkv_ref[...]).astype(BF16)
    d_attn_ref[...] = nt(dy_ref[...], w_out_ref[...]).astype(BF16)

    groups = HEADS // GROUP

    @pl.loop(0, (TOKENS // WINDOW) * groups)
    def _(step):
        attention_group(
            step // groups, step % groups, last, qkv_ref, d_attn_ref, attended_ref, dqkv_ref
        )

    dhidden = nt(dqkv_ref[...], w_qkv_ref[...])
    normed = normed_ref[...]
    gain_local = jnp.sum(dhidden * normed, axis=0, keepdims=True)
    dnorm = dhidden * gain_ref[...]
    drolled = dy_ref[...].astype(F32) + inverse * (
        dnorm
        - jnp.mean(dnorm, axis=-1, keepdims=True)
        - normed * jnp.mean(dnorm * normed, axis=-1, keepdims=True)
    )
    drolled_ref[...] = drolled.astype(BF16)
    back_ref[0:72, :] = drolled[72:144].astype(BF16)
    back_ref[72:144, :] = drolled[180:252].astype(BF16)

    coarse = gain_local.astype(BF16)
    fine = (gain_local - coarse.astype(F32)).astype(BF16)
    rows = [part[:, 128 * j : 128 * (j + 1)] for part in (coarse, fine) for j in range(4)]
    gain_tile_ref[...] = jnp.concatenate(
        [row.astype(F32) for row in rows] + [jnp.zeros((8, 128), F32)], axis=0
    ).astype(BF16)


def block(place, tokens, grads, norm_gain, w_qkv, w_out):
    feature = HEADS * HEAD_DIM
    vmem = pl.BlockSpec(memory_space=pltpu.VMEM)

    def half(width):
        return jax.ShapeDtypeStruct((TOKENS, width), BF16)

    return pl.pallas_call(
        block_kernel,
        out_shape=(
            half(feature), jax.ShapeDtypeStruct((WINDOW, feature), BF16),
            half(feature), half(3 * feature), half(feature),
            jax.ShapeDtypeStruct((16, 128), BF16),
        ),
        in_specs=[pl.BlockSpec(memory_space=pltpu.SMEM)] + [vmem] * 5,
        out_specs=(vmem,) * 6,
        scratch_shapes=[
            pltpu.VMEM((TOKENS, feature), F32),
            pltpu.VMEM((TOKENS, 3 * feature), BF16),
            pltpu.VMEM((TOKENS, feature), BF16),
        ],
        compiler_params=pltpu.CompilerParams(vmem_limit_bytes=40 * 1024 * 1024),
        cost_estimate=pl.CostEstimate(
            flops=2_000_000_000, bytes_accessed=6_000_000, transcendentals=700_000
        ),
        name="window_block",
    )(place, tokens, grads, norm_gain, w_qkv, w_out)


def weights_kernel(
    place, hidden_ref, dqkv_ref, attended_ref, dy_ref, gain_tile_ref, keep_ref, send_ref, total_ref
):
    core = place[1]
    feature = HEADS * HEAD_DIM
    total_ref[:, 0 : 3 * feature] = tn(hidden_ref[...], dqkv_ref[...]).astype(BF16)
    total_ref[:, 3 * feature : 4 * feature] = tn(attended_ref[...], dy_ref[...]).astype(BF16)

    @pl.loop(0, 16)
    def _(chunk):
        for half, out in ((core, keep_ref), (1 - core, send_ref)):
            start = pl.multiple_of(half * 256 + chunk * 16, 16)
            rows = total_ref[pl.ds(start, 16), :]
            for j in range(16):
                out[chunk, j] = rows[:, 128 * j : 128 * (j + 1)]
            out[chunk, 16] = gain_tile_ref[...]


def weight_terms(place, hidden, dqkv, attended, grads, gain_tile):
    feature = HEADS * HEAD_DIM
    vmem = pl.BlockSpec(memory_space=pltpu.VMEM)
    chunks = jax.ShapeDtypeStruct((16, 17, 16, 128), BF16)
    return pl.pallas_call(
        weights_kernel,
        out_shape=(chunks, chunks),
        in_specs=[pl.BlockSpec(memory_space=pltpu.SMEM)] + [vmem] * 5,
        out_specs=(vmem, vmem),
        scratch_shapes=[pltpu.VMEM((feature, 4 * feature), BF16)],
        compiler_params=pltpu.CompilerParams(vmem_limit_bytes=40 * 1024 * 1024),
        cost_estimate=pl.CostEstimate(
            flops=40_000_000_000, bytes_accessed=100_000_000, transcendentals=0
        ),
        name="weight_terms",
    )(place, hidden, dqkv, attended, grads, gain_tile)


def index(zh, y, x, zl, c):
    return (((zh * 4 + y) * 4 + x) * 8 + zl) * 2 + c


def in_one_piece(work, start):
    once = jnp.minimum(lax.axis_index(LAT) + 1, 1)

    def body(turn, values):
        values, _ = lax.optimization_barrier((values, turn))
        return work(*values)

    return lax.fori_loop(0, once, body, start)


def middle_of(zh, lat):
    zl, c = lat // 2, lat % 2
    y, x = MIDS[(zl % 2) * 2 + c]
    return index(zh, y, x, zl, c)


def fetch(blocks, corner, top):
    out, out_corner, onward = [], [], []
    for zh in range(2):
        for lat in range(16):
            middle, target = middle_of(zh, lat), index(1 - zh, 3, 3, lat // 2, lat % 2)
            out.append((index(zh, 0, 0, lat // 2, lat % 2), middle))
            onward.append((middle, target))
            if lat < 15:
                out_corner.append((index(zh, 0, 0, (lat + 1) // 2, (lat + 1) % 2), middle))
            else:
                out_corner.append((index(zh, 0, 0, 0, 0), target))
    halfway = lax.ppermute(blocks, ALL, out)
    halfway_corner = lax.ppermute(corner, ALL, out_corner)
    halfway, halfway_corner, blocks, corner, top = lax.optimization_barrier(
        (halfway, halfway_corner, blocks, corner, top)
    )
    crossed = [
        lax.ppermute(part, ALL, onward)
        for part in (halfway[:2], jnp.stack([halfway[2], halfway_corner]))
    ]
    inner = [i for i in range(32) if i % 16 < 15]

    def usual(blocks, corner, top):
        return (
            lax.ppermute(blocks, LON, [(i + 1, i) for i in inner]),
            lax.ppermute(
                corner, ALL,
                [((i + 1) * 16 + (j + 1) % 16, i * 16 + j) for i in inner for j in range(16)],
            ),
            lax.ppermute(top, LAT, [((i + 1) % 16, i) for i in range(16)]),
        )

    normal, normal_corner, lat_block = in_one_piece(usual, (blocks, corner, top))
    *crossed, normal, normal_corner, lat_block = lax.optimization_barrier(
        (*crossed, normal, normal_corner, lat_block)
    )
    east = lax.axis_index(LON) % 16 == 15
    last = lax.axis_index(LAT) == 15
    across = (crossed[0][0], crossed[0][1], crossed[1][0])
    arrived = [jnp.where(east, across[k], normal[k]) for k in range(3)]
    over = jnp.where(last, halfway_corner, crossed[1][1])
    return arrived + [jnp.where(east, over, normal_corner)], lat_block


def per_device(block_input, cotangent, norm_gain, w_qkv, w_out):
    half_lat, half_lon = WLAT // 2, WLON // 2
    levels, lat_rows, lon_cols, feature = block_input.shape
    stacked = jnp.stack([block_input, cotangent])

    def part(row, col):
        return stacked[:, :, row : row + half_lat, col : col + half_lon].reshape(2, BLOCK, feature)

    west = jnp.stack([part(row, 0) for row in (3, 6, 9)])
    (p0, p1, p2, corner), lat_block = fetch(west, part(0, 0), part(0, half_lon))
    own = [part(row, half_lon) for row in (3, 6, 9)]
    tokens = jnp.concatenate([own[0], own[1], p0, p1, own[2], p2, corner, lat_block], axis=1)
    last = lax.axis_index(LAT) == 15
    place = jnp.stack([last, lax.axis_index("c")]).astype(jnp.int32)
    drolled, back, hidden, dqkv, attended, gain_tile = block(
        place, tokens[0], tokens[1], norm_gain.reshape(1, feature), w_qkv, w_out
    )

    back_lon = lax.ppermute(back, LON, [(i, (i + 1) % 32) for i in range(32)])

    def sum_in_plane(hidden, dqkv, attended, grads, gain_tile, _):
        keep, send = weight_terms(place, hidden, dqkv, attended, grads, gain_tile)
        other = lax.ppermute(send, "c", [(0, 1), (1, 0)])
        pair = (keep.astype(F32) + other.astype(F32)).astype(BF16)
        plane = lax.all_to_all(pair, ("y", "x"), 0, 0, tiled=True)
        return hidden, dqkv, attended, grads, gain_tile, jnp.sum(plane.astype(F32), axis=0)

    nothing = jnp.zeros((17, 16, 128), F32)
    *_, plane = in_one_piece(
        sum_in_plane, (hidden, dqkv, attended, tokens[1], gain_tile, nothing)
    )
    plane, back_lon = lax.optimization_barrier((plane, back_lon))
    back_lat = lax.ppermute(
        jnp.stack([drolled[252:288], back_lon[108:144]]), LAT,
        [(i, (i + 1) % 16) for i in range(16)],
    )
    gain_part = jnp.broadcast_to(plane[16].astype(BF16), (16, 16, 128))
    column = lax.all_to_all(
        jnp.stack([plane[:16].astype(BF16), gain_part], axis=1), ("zh", "zl"), 0, 0, tiled=True
    )
    column = jnp.sum(column.astype(F32), axis=0)
    gain_rows = column[1]
    gain_grad = (gain_rows[0:4] + gain_rows[4:8]).reshape(feature)
    final = column[0].astype(BF16)
    fan = jnp.broadcast_to(final, (32, 16, 128))
    gathered = lax.all_to_all(fan, ("zh", "zl", "c"), 0, 0, tiled=True)
    gathered = gathered.reshape(16, 2, 16, 128)
    mine = lax.dynamic_index_in_dim(gathered, lax.axis_index("zh"), axis=1, keepdims=False)
    weights = mine.transpose(1, 0, 2).reshape(16, 4 * feature).astype(F32)

    def grid(piece):
        return piece.reshape(levels, half_lat, half_lon, feature)

    rows = [
        (back_lat[1], back_lat[0]),
        (back_lon[0:36], drolled[0:36]),
        (back_lon[36:72], drolled[36:72]),
        (back_lon[72:108], drolled[144:180]),
    ]
    input_grad = jnp.concatenate(
        [jnp.concatenate([grid(west), grid(east)], axis=2) for west, east in rows], axis=1
    )
    return input_grad, weights[:, : 3 * feature], weights[:, 3 * feature :], gain_grad


def solution(mesh):
    fine = Mesh(mesh.devices.reshape(2, 4, 4, 8, 2), ALL)
    grid_spec = P(None, LAT, LON, None)
    return jax.shard_map(
        per_device,
        mesh=fine,
        in_specs=(grid_spec, grid_spec, P(), P(), P()),
        out_specs=(grid_spec, P(LON, None), P(LON, None), P()),
        check_vma=False,
    )
```

```python
import functools
import math

import jax
import jax.numpy as jnp
from jax import lax
from jax.experimental import pallas as pl
from jax.experimental.pallas import tpu as pltpu
from jax.sharding import Mesh, PartitionSpec as P

HEADS = 16
HEAD_DIM = 32
WLAT = 6
WLON = 12
WINDOW = 144
TOKENS = 288
HALF = 72
EXTRA = 80
ALL_TOKENS = TOKENS + EXTRA
BLOCK = 36
GROUP = 4
BF16 = jnp.bfloat16
F32 = jnp.float32
LON = ("zh", "y", "x")
LAT = ("zl", "c")
ALL = LON + LAT
MIDS = ((0, 3), (3, 0), (3, 1), (1, 3), (2, 0), (0, 2), (1, 0), (2, 3))


def nn(a, b):
    return lax.dot_general(a, b, (((1,), (0,)), ((), ())), preferred_element_type=F32)


def nt(a, b):
    return lax.dot_general(a, b, (((1,), (1,)), ((), ())), preferred_element_type=F32)


def tn(a, b):
    return lax.dot_general(a, b, (((0,), (0,)), ((), ())), preferred_element_type=F32)


def attention_group(start, size, masked, group, qkv, d_attn, attended, dqkv):
    feature = HEADS * HEAD_DIM
    width = GROUP * HEAD_DIM
    rows = pl.ds(start, size)
    at = group * width

    def columns(offset):
        return pl.ds(pl.multiple_of(at + offset, 128), width)

    queries = qkv[rows, columns(0)]
    keys = qkv[rows, columns(feature)]
    values = qkv[rows, columns(2 * feature)]
    grads = d_attn[rows, columns(0)]
    scale = 1.0 / math.sqrt(HEAD_DIM)
    lane_head = lax.broadcasted_iota(jnp.int32, (1, width), 1) // HEAD_DIM
    key_late = lax.broadcasted_iota(jnp.int32, (size, size), 0) >= HALF
    query_late = lax.broadcasted_iota(jnp.int32, (size, size), 1) >= HALF
    allowed = jnp.logical_or(key_late == query_late, jnp.logical_not(masked))

    own = [(lane_head == head).astype(BF16) for head in range(GROUP)]
    key_stack = jnp.concatenate([keys * mask for mask in own], axis=0)
    value_stack = jnp.concatenate([values * mask for mask in own], axis=0)
    scores_all = nt(key_stack, queries)
    dprob_all = nt(value_stack, grads)
    prob_parts, dscore_parts = [], []
    for head in range(GROUP):
        part = slice(head * size, (head + 1) * size)
        scores = jnp.where(allowed, scores_all[part] * (scale * math.log2(math.e)), -jnp.inf)
        weights = jnp.exp2(scores - jnp.max(scores, axis=0, keepdims=True))
        prob = weights * (1.0 / jnp.sum(weights, axis=0, keepdims=True))
        dprob = dprob_all[part]
        delta = jnp.sum(prob * dprob, axis=0, keepdims=True)
        dscore_parts.append((prob * (dprob - delta) * scale).astype(BF16))
        prob_parts.append(prob.astype(BF16))
    prob_all = jnp.concatenate(prob_parts, axis=0)
    dscore_all = jnp.concatenate(dscore_parts, axis=0)

    def own_columns(stack):
        picked = stack[0:size]
        for head in range(1, GROUP):
            picked = jnp.where(lane_head == head, stack[head * size : (head + 1) * size], picked)
        return picked.astype(BF16)

    attended[rows, columns(0)] = tn(prob_all, value_stack).astype(BF16)
    dqkv[rows, columns(0)] = tn(dscore_all, key_stack).astype(BF16)
    dqkv[rows, columns(feature)] = own_columns(nn(dscore_all, queries))
    dqkv[rows, columns(2 * feature)] = own_columns(nn(prob_all, grads))


def block_kernel(
    place, x_ref, dy_ref, gain_ref, w_qkv_ref, w_out_ref,
    drolled_ref, back_ref, hidden_ref, dqkv_ref, attended_ref, gain_tile_ref,
    normed_ref, inverse_ref, qkv_ref, d_attn_ref, gain_sum_ref,
):
    first = place[0]
    last = place[1]
    feature = HEADS * HEAD_DIM
    regular = pl.ds(0, TOKENS)
    extra = pl.ds(TOKENS, EXTRA)

    def project(rows):
        values = x_ref[rows, :].astype(F32)
        centred = values - jnp.mean(values, axis=-1, keepdims=True)
        inverse = lax.rsqrt(jnp.mean(centred * centred, axis=-1, keepdims=True) + 1e-05)
        normed = centred * inverse
        normed_ref[rows, :] = normed
        inverse_ref[rows, :] = jnp.broadcast_to(inverse, (inverse.shape[0], 128))
        hidden = (normed * gain_ref[...]).astype(BF16)
        hidden_ref[rows, :] = hidden
        qkv_ref[rows, :] = nn(hidden, w_qkv_ref[...]).astype(BF16)
        d_attn_ref[rows, :] = nt(dy_ref[rows, :], w_out_ref[...]).astype(BF16)

    def finish(rows):
        dhidden = nt(dqkv_ref[rows, :], w_qkv_ref[...])
        normed = normed_ref[rows, :]
        dnorm = dhidden * gain_ref[...]
        drolled = dy_ref[rows, :].astype(F32) + inverse_ref[rows, 0:1] * (
            dnorm
            - jnp.mean(dnorm, axis=-1, keepdims=True)
            - normed * jnp.mean(dnorm * normed, axis=-1, keepdims=True)
        )
        drolled_ref[rows, :] = drolled.astype(BF16)
        return drolled, jnp.sum(dhidden * normed, axis=0, keepdims=True)

    @pl.when(first == 1)
    def _():
        project(pl.ds(0, ALL_TOKENS))

    @pl.when(first == 0)
    def _():
        project(regular)
        hidden_ref[extra, :] = jnp.zeros((EXTRA, feature), BF16)
        attended_ref[extra, :] = jnp.zeros((EXTRA, feature), BF16)
        dqkv_ref[extra, :] = jnp.zeros((EXTRA, 3 * feature), BF16)
        drolled_ref[extra, :] = jnp.zeros((EXTRA, feature), BF16)

    groups = HEADS // GROUP

    @pl.loop(0, (TOKENS // WINDOW) * groups)
    def _(step):
        window = step // groups
        attention_group(
            pl.multiple_of(window * WINDOW, 16), WINDOW,
            jnp.logical_and(last == 1, window == 1), step % groups,
            qkv_ref, d_attn_ref, attended_ref, dqkv_ref,
        )

    def hand_back(drolled):
        back_ref[0:72, :] = drolled[72:144].astype(BF16)
        back_ref[72:144, :] = drolled[180:252].astype(BF16)

    @pl.when(first == 0)
    def _():
        drolled, gain_sum = finish(regular)
        gain_sum_ref[...] = gain_sum
        hand_back(drolled)
        back_ref[144:180, :] = jnp.zeros((BLOCK, feature), BF16)

    @pl.when(first == 1)
    def _():
        @pl.loop(0, groups)
        def _(group):
            attention_group(
                TOKENS, EXTRA, first == 1, group, qkv_ref, d_attn_ref, attended_ref, dqkv_ref
            )

        drolled, gain_sum = finish(pl.ds(0, ALL_TOKENS))
        gain_sum_ref[...] = gain_sum
        hand_back(drolled)
        back_ref[144:180, :] = drolled[324:360].astype(BF16)

    gain_local = gain_sum_ref[...]
    coarse = gain_local.astype(BF16)
    fine = (gain_local - coarse.astype(F32)).astype(BF16)
    rows = [part[:, 128 * j : 128 * (j + 1)] for part in (coarse, fine) for j in range(4)]
    gain_tile_ref[...] = jnp.concatenate(
        [row.astype(F32) for row in rows] + [jnp.zeros((8, 128), F32)], axis=0
    ).astype(BF16)


def block(place, tokens, grads, norm_gain, w_qkv, w_out):
    feature = HEADS * HEAD_DIM
    vmem = pl.BlockSpec(memory_space=pltpu.VMEM)

    def half(rows, width):
        return jax.ShapeDtypeStruct((rows, width), BF16)

    return pl.pallas_call(
        block_kernel,
        out_shape=(
            half(ALL_TOKENS, feature), half(5 * BLOCK, feature),
            half(ALL_TOKENS, feature), half(ALL_TOKENS, 3 * feature), half(ALL_TOKENS, feature),
            half(16, 128),
        ),
        in_specs=[pl.BlockSpec(memory_space=pltpu.SMEM)] + [vmem] * 5,
        out_specs=(vmem,) * 6,
        scratch_shapes=[
            pltpu.VMEM((ALL_TOKENS, feature), F32),
            pltpu.VMEM((ALL_TOKENS, 128), F32),
            pltpu.VMEM((ALL_TOKENS, 3 * feature), BF16),
            pltpu.VMEM((ALL_TOKENS, feature), BF16),
            pltpu.VMEM((1, feature), F32),
        ],
        compiler_params=pltpu.CompilerParams(vmem_limit_bytes=40 * 1024 * 1024),
        cost_estimate=pl.CostEstimate(
            flops=2_000_000_000, bytes_accessed=6_000_000, transcendentals=700_000
        ),
        name="window_block",
    )(place, tokens, grads, norm_gain, w_qkv, w_out)


def weights_kernel(
    place, hidden_ref, dqkv_ref, attended_ref, dy_ref, gain_tile_ref, keep_ref, send_ref, total_ref
):
    core = place[2]
    feature = HEADS * HEAD_DIM
    total_ref[:, 0 : 3 * feature] = tn(hidden_ref[...], dqkv_ref[...]).astype(BF16)
    total_ref[:, 3 * feature : 4 * feature] = tn(attended_ref[...], dy_ref[...]).astype(BF16)

    @pl.loop(0, 16)
    def _(chunk):
        for half, out in ((core, keep_ref), (1 - core, send_ref)):
            start = pl.multiple_of(half * 256 + chunk * 16, 16)
            rows = total_ref[pl.ds(start, 16), :]
            for j in range(16):
                out[chunk, j] = rows[:, 128 * j : 128 * (j + 1)]
            out[chunk, 16] = gain_tile_ref[...]


def weight_terms(place, hidden, dqkv, attended, grads, gain_tile):
    feature = HEADS * HEAD_DIM
    vmem = pl.BlockSpec(memory_space=pltpu.VMEM)
    chunks = jax.ShapeDtypeStruct((16, 17, 16, 128), BF16)
    return pl.pallas_call(
        weights_kernel,
        out_shape=(chunks, chunks),
        in_specs=[pl.BlockSpec(memory_space=pltpu.SMEM)] + [vmem] * 5,
        out_specs=(vmem, vmem),
        scratch_shapes=[pltpu.VMEM((feature, 4 * feature), BF16)],
        compiler_params=pltpu.CompilerParams(vmem_limit_bytes=40 * 1024 * 1024),
        cost_estimate=pl.CostEstimate(
            flops=40_000_000_000, bytes_accessed=100_000_000, transcendentals=0
        ),
        name="weight_terms",
    )(place, hidden, dqkv, attended, grads, gain_tile)


def small_call(body, name, out_shape, *operands, place=None):
    vmem = pl.BlockSpec(memory_space=pltpu.VMEM)
    many = isinstance(out_shape, tuple)
    head = () if place is None else (place,)
    return pl.pallas_call(
        body,
        out_shape=out_shape,
        in_specs=[pl.BlockSpec(memory_space=pltpu.SMEM)] * len(head) + [vmem] * len(operands),
        out_specs=(vmem,) * len(out_shape) if many else vmem,
        compiler_params=pltpu.CompilerParams(vmem_limit_bytes=16 * 1024 * 1024),
        name=name,
    )(*head, *operands)


def pair_kernel(keep_ref, other_ref, out_ref):
    @pl.loop(0, 16)
    def _(chunk):
        for j in range(17):
            total = keep_ref[chunk, j].astype(F32) + other_ref[chunk, j].astype(F32)
            out_ref[chunk, j] = total.astype(BF16)


def plane_kernel(parts_ref, out_ref):
    gain = parts_ref[0, 16].astype(F32)
    for chunk in range(1, 16):
        gain = gain + parts_ref[chunk, 16].astype(F32)

    @pl.loop(0, 16)
    def _(j):
        total = parts_ref[0, j].astype(F32)
        for chunk in range(1, 16):
            total = total + parts_ref[chunk, j].astype(F32)
        out_ref[j, 0] = total.astype(BF16)
        out_ref[j, 1] = gain.astype(BF16)


def column_kernel(parts_ref, fan_ref, gain_ref):
    total = parts_ref[0, 0].astype(F32)
    gain = parts_ref[0, 1].astype(F32)
    for z in range(1, 16):
        total = total + parts_ref[z, 0].astype(F32)
        gain = gain + parts_ref[z, 1].astype(F32)
    total = total.astype(BF16)
    for peer in range(32):
        fan_ref[peer] = total
    gain_ref[...] = gain[0:4] + gain[4:8]


def spread_kernel(place, tiles_ref, qkv_ref, out_ref):
    half = place[3]
    for z in range(16):
        tile = tiles_ref[z, half].astype(F32)
        if z < 12:
            qkv_ref[:, 128 * z : 128 * (z + 1)] = tile
        else:
            out_ref[:, 128 * (z - 12) : 128 * (z - 11)] = tile


def index(zh, y, x, zl, c):
    return (((zh * 4 + y) * 4 + x) * 8 + zl) * 2 + c


def in_one_piece(work, start):
    once = jnp.minimum(lax.axis_index(LAT) + 1, 1)

    def body(turn, values):
        values, _ = lax.optimization_barrier((values, turn))
        return work(*values)

    return lax.fori_loop(0, once, body, start)


def middle_of(zh, lat):
    zl, c = lat // 2, lat % 2
    y, x = MIDS[zl]
    z = (zh * 8 + zl + 1 - 2 * c) % 16
    return index(z // 8, y, x, z % 8, c)


def fetch(blocks, corner, top, first_block):
    out, out_corner, onward = [], [], []
    for zh in range(2):
        for lat in range(16):
            middle, target = middle_of(zh, lat), index(1 - zh, 3, 3, lat // 2, lat % 2)
            out.append((index(zh, 0, 0, lat // 2, lat % 2), middle))
            onward.append((middle, target))
            if lat < 15:
                out_corner.append((index(zh, 0, 0, (lat + 1) // 2, (lat + 1) % 2), middle))
    halfway = lax.ppermute(blocks, ALL, out)
    halfway_corner = lax.ppermute(corner, ALL, out_corner)
    halfway, halfway_corner, blocks, corner, top, first_block = lax.optimization_barrier(
        (halfway, halfway_corner, blocks, corner, top, first_block)
    )
    crossed = lax.ppermute(jnp.concatenate([halfway, halfway_corner[None]]), ALL, onward)
    inner = [i for i in range(32) if i % 16 < 15]

    def usual(blocks, corner, top, first_block):
        return (
            lax.ppermute(blocks, LON, [(i + 1, i) for i in inner]),
            lax.ppermute(
                corner, ALL, [((i + 1) * 16 + j + 1, i * 16 + j) for i in inner for j in range(15)]
            ),
            lax.ppermute(top, LAT, [(j + 1, j) for j in range(15)]),
            lax.ppermute(first_block, ALL, [((i + 1) % 32 * 16, i * 16) for i in range(32)]),
        )

    usual_blocks = in_one_piece(usual, (blocks, corner, top, first_block))
    crossed, normal, normal_corner, lat_block, extra = lax.optimization_barrier(
        (crossed, *usual_blocks)
    )
    east = lax.axis_index(LON) % 16 == 15
    arrived = [jnp.where(east, crossed[k], normal[k]) for k in range(3)]
    return arrived + [jnp.where(east, crossed[3], normal_corner)], lat_block, extra


def per_device(block_input, cotangent, norm_gain, w_qkv, w_out):
    half_lat, half_lon = WLAT // 2, WLON // 2
    levels, lat_rows, lon_cols, feature = block_input.shape
    stacked = jnp.stack([block_input, cotangent])

    def part(row, col):
        return stacked[:, :, row : row + half_lat, col : col + half_lon].reshape(2, BLOCK, feature)

    west = jnp.stack([part(row, 0) for row in (3, 6, 9)])
    (p0, p1, p2, corner), lat_block, extra = fetch(
        west, part(0, 0), part(0, half_lon), part(0, 0)
    )
    own = [part(row, half_lon) for row in (3, 6, 9, 0)]
    none = jnp.zeros((2, EXTRA - HALF, feature), BF16)
    tokens = jnp.concatenate(
        [own[0], own[1], p0, p1, own[2], p2, corner, lat_block, own[3], extra, none], axis=1
    )
    lat = lax.axis_index(LAT)
    first = lat == 0
    place = jnp.stack([first, lat == 15, lax.axis_index("c"), lax.axis_index("zh")])
    place = place.astype(jnp.int32)
    drolled, back, hidden, dqkv, attended, gain_tile = block(
        place, tokens[0], tokens[1], norm_gain.reshape(1, feature), w_qkv, w_out
    )

    back_lon = lax.ppermute(back, LON, [(i, (i + 1) % 32) for i in range(32)])

    def sum_in_plane(hidden, dqkv, attended, grads, gain_tile, _):
        keep, send = weight_terms(place, hidden, dqkv, attended, grads, gain_tile)
        other = lax.ppermute(send, "c", [(0, 1), (1, 0)])
        pair = small_call(
            pair_kernel, "pair_sum", jax.ShapeDtypeStruct(keep.shape, BF16), keep, other
        )
        plane = lax.all_to_all(pair, ("y", "x"), 0, 0, tiled=True)
        plane = small_call(
            plane_kernel, "plane_sum", jax.ShapeDtypeStruct((16, 2, 16, 128), BF16), plane
        )
        return hidden, dqkv, attended, grads, gain_tile, plane

    nothing = jnp.zeros((16, 2, 16, 128), BF16)
    *_, plane = in_one_piece(
        sum_in_plane, (hidden, dqkv, attended, tokens[1], gain_tile, nothing)
    )
    plane, back_lon = lax.optimization_barrier((plane, back_lon))
    back_lat = lax.ppermute(
        jnp.stack([drolled[252:288], back_lon[108:144]]), LAT, [(j, j + 1) for j in range(15)]
    )
    column = lax.all_to_all(plane, ("zh", "zl"), 0, 0, tiled=True)
    fan, gain_rows = small_call(
        column_kernel, "column_sum",
        (jax.ShapeDtypeStruct((32, 16, 128), BF16), jax.ShapeDtypeStruct((4, 128), F32)),
        column,
    )
    gain_grad = gain_rows.reshape(feature)
    gathered = lax.all_to_all(fan, ("zh", "zl", "c"), 0, 0, tiled=True)
    qkv_grad, out_grad = small_call(
        spread_kernel, "spread",
        (
            jax.ShapeDtypeStruct((16, 3 * feature), F32),
            jax.ShapeDtypeStruct((16, feature), F32),
        ),
        gathered.reshape(16, 2, 16, 128), place=place,
    )

    def grid(piece):
        return piece.reshape(levels, half_lat, half_lon, feature)

    rows = [
        (jnp.where(first, back_lon[144:180], back_lat[1]), jnp.where(first, drolled[288:324], back_lat[0])),
        (back_lon[0:36], drolled[0:36]),
        (back_lon[36:72], drolled[36:72]),
        (back_lon[72:108], drolled[144:180]),
    ]
    input_grad = jnp.concatenate(
        [jnp.concatenate([grid(west), grid(east)], axis=2) for west, east in rows], axis=1
    )
    return input_grad, qkv_grad, out_grad, gain_grad


def solution(mesh):
    fine = Mesh(mesh.devices.reshape(2, 4, 4, 8, 2), ALL)
    grid_spec = P(None, LAT, LON, None)
    return jax.shard_map(
        per_device,
        mesh=fine,
        in_specs=(grid_spec, grid_spec, P(), P(), P()),
        out_specs=(grid_spec, P(LON, None), P(LON, None), P()),
        check_vma=False,
    )
```

```python
import functools
import math

import jax
import jax.numpy as jnp
from jax import lax
from jax.experimental import pallas as pl
from jax.experimental.pallas import tpu as pltpu
from jax.sharding import Mesh, PartitionSpec as P

HEADS = 16
HEAD_DIM = 32
WLAT = 6
WLON = 12
WINDOW = 144
TOKENS = 288
HALF = 72
EXTRA = 80
ALL_TOKENS = TOKENS + EXTRA
BLOCK = 36
GROUP = 4
BF16 = jnp.bfloat16
F32 = jnp.float32
LON = ("zh", "y", "x")
LAT = ("zq", "zb", "c")
ALONG_Z = ("zh", "zq", "zb")
ALL = LON + LAT
MIDS = ((0, 3), (3, 0), (3, 1), (1, 3), (2, 0), (0, 2), (1, 0), (2, 3))


def nn(a, b):
    return lax.dot_general(a, b, (((1,), (0,)), ((), ())), preferred_element_type=F32)


def nt(a, b):
    return lax.dot_general(a, b, (((1,), (1,)), ((), ())), preferred_element_type=F32)


def tn(a, b):
    return lax.dot_general(a, b, (((0,), (0,)), ((), ())), preferred_element_type=F32)


def attention_group(start, size, masked, group, qkv, d_attn, attended_t, dqkv):
    feature = HEADS * HEAD_DIM
    width = GROUP * HEAD_DIM
    rows = pl.ds(start, size)
    at = group * width

    def columns(offset):
        return pl.ds(pl.multiple_of(at + offset, 128), width)

    queries = qkv[rows, columns(0)]
    keys = qkv[rows, columns(feature)]
    values = qkv[rows, columns(2 * feature)]
    grads = d_attn[rows, columns(0)]
    scale = 1.0 / math.sqrt(HEAD_DIM)
    lane_head = lax.broadcasted_iota(jnp.int32, (1, width), 1) // HEAD_DIM
    key_late = lax.broadcasted_iota(jnp.int32, (size, size), 0) >= HALF
    query_late = lax.broadcasted_iota(jnp.int32, (size, size), 1) >= HALF
    allowed = jnp.logical_or(key_late == query_late, jnp.logical_not(masked))

    own = [(lane_head == head).astype(BF16) for head in range(GROUP)]
    key_stack = jnp.concatenate([keys * mask for mask in own], axis=0)
    value_stack = jnp.concatenate([values * mask for mask in own], axis=0)
    scores_all = nt(key_stack, queries)
    dprob_all = nt(value_stack, grads)
    prob_parts, dscore_parts = [], []
    for head in range(GROUP):
        part = slice(head * size, (head + 1) * size)
        scores = jnp.where(allowed, scores_all[part] * (scale * math.log2(math.e)), -jnp.inf)
        weights = jnp.exp2(scores - jnp.max(scores, axis=0, keepdims=True))
        prob = weights * (1.0 / jnp.sum(weights, axis=0, keepdims=True))
        dprob = dprob_all[part]
        delta = jnp.sum(prob * dprob, axis=0, keepdims=True)
        dscore_parts.append((prob * (dprob - delta) * scale).astype(BF16))
        prob_parts.append(prob.astype(BF16))
    prob_all = jnp.concatenate(prob_parts, axis=0)
    dscore_all = jnp.concatenate(dscore_parts, axis=0)

    def own_columns(stack):
        picked = stack[0:size]
        for head in range(1, GROUP):
            picked = jnp.where(lane_head == head, stack[head * size : (head + 1) * size], picked)
        return picked.astype(BF16)

    def turned(array):
        return array.astype(F32).T.astype(BF16)

    def by_head(heads_t, parts):
        return jnp.concatenate(
            [
                nn(heads_t[head * HEAD_DIM : (head + 1) * HEAD_DIM], parts[head])
                for head in range(GROUP)
            ],
            axis=0,
        )

    attended_t[pl.ds(pl.multiple_of(at, 128), width), :] = by_head(
        turned(values), prob_parts
    ).astype(BF16)
    dqkv[rows, columns(0)] = by_head(turned(keys), dscore_parts).T.astype(BF16)
    dqkv[rows, columns(feature)] = own_columns(nn(dscore_all, queries))
    dqkv[rows, columns(2 * feature)] = own_columns(nn(prob_all, grads))


def block_kernel(
    place, own_ref, usual_ref, usual_corner_ref, crossed_ref, lat_ref, extra_ref,
    gain_ref, w_qkv_ref, w_out_ref,
    drolled_ref, back_ref, dy_ref, hidden_ref, dqkv_ref, attended_ref, attended_extra_ref,
    gain_tile_ref, nothing_ref,
    x_ref, dy_wide_ref, normed_ref, inverse_ref, qkv_ref, d_attn_ref,
):
    first = place[0]
    last = place[1]
    east = place[3] == 1
    feature = HEADS * HEAD_DIM
    regular = pl.ds(0, TOKENS)
    extra = pl.ds(TOKENS, EXTRA)

    for kind, ref in ((0, x_ref), (1, dy_wide_ref)):

        def fetched(k, usual):
            return jnp.where(east, crossed_ref[k, kind].astype(F32), usual.astype(F32))

        blocks = (
            own_ref[0, kind], own_ref[1, kind], fetched(0, usual_ref[0, kind]),
            fetched(1, usual_ref[1, kind]), own_ref[2, kind], fetched(2, usual_ref[2, kind]),
            fetched(3, usual_corner_ref[kind]), lat_ref[kind], own_ref[3, kind], extra_ref[kind],
        )
        for at, part in enumerate(blocks):
            ref[at * BLOCK : (at + 1) * BLOCK, :] = part.astype(F32)
        ref[TOKENS + HALF :, :] = jnp.zeros((EXTRA - HALF, feature), F32)
    dy_ref[...] = dy_wide_ref[...].astype(BF16)

    def project(rows):
        values = x_ref[rows, :]
        centred = values - jnp.mean(values, axis=-1, keepdims=True)
        inverse = lax.rsqrt(jnp.mean(centred * centred, axis=-1, keepdims=True) + 1e-05)
        normed = centred * inverse
        normed_ref[rows, :] = normed
        inverse_ref[rows, :] = jnp.broadcast_to(inverse, (inverse.shape[0], 128))
        hidden = (normed * gain_ref[...]).astype(BF16)
        hidden_ref[rows, :] = hidden
        qkv_ref[rows, :] = nn(hidden, w_qkv_ref[...]).astype(BF16)
        d_attn_ref[rows, :] = nt(dy_ref[rows, :], w_out_ref[...]).astype(BF16)

    def finish(rows):
        dhidden = nt(dqkv_ref[rows, :], w_qkv_ref[...])
        normed = normed_ref[rows, :]
        dnorm = dhidden * gain_ref[...]
        drolled = dy_wide_ref[rows, :] + inverse_ref[rows, 0:1] * (
            dnorm
            - jnp.mean(dnorm, axis=-1, keepdims=True)
            - normed * jnp.mean(dnorm * normed, axis=-1, keepdims=True)
        )
        drolled_ref[rows, :] = drolled.astype(BF16)
        back_ref[0:72, :] = drolled[72:144].astype(BF16)
        back_ref[72:144, :] = drolled[180:252].astype(BF16)
        if drolled.shape[0] > TOKENS:
            back_ref[144:180, :] = drolled[324:360].astype(BF16)
        else:
            back_ref[144:180, :] = jnp.zeros((BLOCK, feature), BF16)

        gain_local = jnp.sum(dhidden * normed, axis=0, keepdims=True)
        coarse = gain_local.astype(BF16)
        fine = (gain_local - coarse.astype(F32)).astype(BF16)
        parts = [part[:, 128 * j : 128 * (j + 1)] for part in (coarse, fine) for j in range(4)]
        gain_tile_ref[...] = jnp.concatenate(
            [part.astype(F32) for part in parts], axis=0
        ).astype(BF16)

    groups = HEADS // GROUP

    def attention(windows):
        @pl.loop(0, windows * groups)
        def _(step):
            window = step // groups
            attention_group(
                pl.multiple_of(window * WINDOW, 16), WINDOW,
                jnp.logical_and(last == 1, window == 1), step % groups,
                qkv_ref, d_attn_ref, attended_ref.at[window], dqkv_ref,
            )

    @pl.when(first == 0)
    def _():
        project(regular)
        attention(TOKENS // WINDOW)
        finish(regular)
        hidden_ref[extra, :] = jnp.zeros((EXTRA, feature), BF16)
        attended_extra_ref[...] = jnp.zeros((feature, EXTRA), BF16)
        dqkv_ref[extra, :] = jnp.zeros((EXTRA, 3 * feature), BF16)
        drolled_ref[extra, :] = jnp.zeros((EXTRA, feature), BF16)

    @pl.when(first == 1)
    def _():
        project(pl.ds(0, ALL_TOKENS))
        attention(TOKENS // WINDOW)

        @pl.loop(0, groups)
        def _(group):
            attention_group(
                TOKENS, EXTRA, first == 1, group,
                qkv_ref, d_attn_ref, attended_extra_ref, dqkv_ref,
            )

        finish(pl.ds(0, ALL_TOKENS))

    nothing_ref[...] = jnp.zeros(nothing_ref.shape, BF16)


def block(place, *operands):
    feature = HEADS * HEAD_DIM
    vmem = pl.BlockSpec(memory_space=pltpu.VMEM)

    def half(*shape):
        return jax.ShapeDtypeStruct(shape, BF16)

    return pl.pallas_call(
        block_kernel,
        out_shape=(
            half(ALL_TOKENS, feature), half(5 * BLOCK, feature), half(ALL_TOKENS, feature),
            half(ALL_TOKENS, feature), half(ALL_TOKENS, 3 * feature),
            half(TOKENS // WINDOW, feature, WINDOW), half(feature, EXTRA),
            half(8, 128), half(16, 72, 128),
        ),
        in_specs=[pl.BlockSpec(memory_space=pltpu.SMEM)] + [vmem] * len(operands),
        out_specs=(vmem,) * 9,
        scratch_shapes=[
            pltpu.VMEM((ALL_TOKENS, feature), F32),
            pltpu.VMEM((ALL_TOKENS, feature), F32),
            pltpu.VMEM((ALL_TOKENS, feature), F32),
            pltpu.VMEM((ALL_TOKENS, 128), F32),
            pltpu.VMEM((ALL_TOKENS, 3 * feature), BF16),
            pltpu.VMEM((ALL_TOKENS, feature), BF16),
        ],
        compiler_params=pltpu.CompilerParams(vmem_limit_bytes=40 * 1024 * 1024),
        cost_estimate=pl.CostEstimate(
            flops=2_000_000_000, bytes_accessed=6_000_000, transcendentals=700_000
        ),
        name="window_block",
    )(place, *operands)


def weights_kernel(
    place, hidden_ref, dqkv_ref, attended_ref, attended_extra_ref, dy_ref, gain_tile_ref,
    keep_ref, send_ref, total_ref,
):
    core = place[2]
    feature = HEADS * HEAD_DIM
    total_ref[:, 0 : 3 * feature] = tn(hidden_ref[...], dqkv_ref[...]).astype(BF16)
    out_total = nn(attended_extra_ref[...], dy_ref[TOKENS:, :])
    for window in range(TOKENS // WINDOW):
        rows = slice(window * WINDOW, (window + 1) * WINDOW)
        out_total = out_total + nn(attended_ref[window], dy_ref[rows, :])
    total_ref[:, 3 * feature :] = out_total.astype(BF16)
    for lon in range(16):
        for ref in (keep_ref, send_ref):
            ref[lon, 0, 128:136] = gain_tile_ref[...]
            ref[lon, 1, 128:136] = gain_tile_ref[...]

    def deal(halves):
        @pl.loop(0, 16)
        def _(lon):
            for zh in range(2):
                start = pl.multiple_of(zh * 256 + lon * 16, 16)
                rows = total_ref[pl.ds(start, 16), :]
                for j in range(16):
                    tile = (zh * 4 + j % 4) * 16
                    halves[j // 8][lon, j % 8 // 4, tile : tile + 16] = rows[:, 128 * j : 128 * (j + 1)]

    @pl.when(core == 0)
    def _():
        deal((keep_ref, send_ref))

    @pl.when(core == 1)
    def _():
        deal((send_ref, keep_ref))


def weight_terms(place, *operands):
    feature = HEADS * HEAD_DIM
    vmem = pl.BlockSpec(memory_space=pltpu.VMEM)
    dealt = jax.ShapeDtypeStruct((16, 2, 136, 128), BF16)
    return pl.pallas_call(
        weights_kernel,
        out_shape=(dealt, dealt),
        in_specs=[pl.BlockSpec(memory_space=pltpu.SMEM)] + [vmem] * len(operands),
        out_specs=(vmem, vmem),
        scratch_shapes=[pltpu.VMEM((feature, 4 * feature), BF16)],
        compiler_params=pltpu.CompilerParams(vmem_limit_bytes=40 * 1024 * 1024),
        cost_estimate=pl.CostEstimate(
            flops=700_000_000, bytes_accessed=4_000_000, transcendentals=0
        ),
        name="weight_terms",
    )(place, *operands)


def small_call(body, name, out_shape, *operands, place=None):
    vmem = pl.BlockSpec(memory_space=pltpu.VMEM)
    many = isinstance(out_shape, tuple)
    head = () if place is None else (place,)
    return pl.pallas_call(
        body,
        out_shape=out_shape,
        in_specs=[pl.BlockSpec(memory_space=pltpu.SMEM)] * len(head) + [vmem] * len(operands),
        out_specs=(vmem,) * len(out_shape) if many else vmem,
        compiler_params=pltpu.CompilerParams(vmem_limit_bytes=8 * 1024 * 1024),
        name=name,
    )(*head, *operands)


def pack_kernel(x_ref, dy_ref, west_ref, corner_ref, top_ref, own_ref, wide_ref):
    for kind, ref in ((0, x_ref), (1, dy_ref)):
        for band in range(4):
            for side in range(2):
                at = (kind * 4 + band) * 2 + side
                for i in range(BLOCK // 2):
                    pair = ref[band * 3 + i // 6, side * 6 + i % 6]
                    wide_ref[at, 2 * i : 2 * i + 2, :] = pair.astype(F32)
                part = wide_ref[at].astype(BF16)
                if side == 1:
                    own_ref[(band + 3) % 4, kind] = part
                    if band == 0:
                        top_ref[kind] = part
                elif band == 0:
                    corner_ref[kind] = part
                else:
                    west_ref[band - 1, kind] = part


def pack(block_input, cotangent):
    feature = block_input.shape[-1]
    vmem = pl.BlockSpec(memory_space=pltpu.VMEM)

    def blocks(*lead):
        return jax.ShapeDtypeStruct((*lead, 2, BLOCK, feature), BF16)

    return pl.pallas_call(
        pack_kernel,
        out_shape=(blocks(3), blocks(), blocks(), blocks(4)),
        in_specs=[vmem] * 2,
        out_specs=(vmem,) * 4,
        scratch_shapes=[pltpu.VMEM((16, BLOCK, feature), F32)],
        compiler_params=pltpu.CompilerParams(vmem_limit_bytes=16 * 1024 * 1024),
        name="pack",
    )(block_input.transpose(1, 2, 0, 3), cotangent.transpose(1, 2, 0, 3))


def pair_kernel(keep_ref, other_ref, out_ref):
    @pl.loop(0, 32)
    def _(chunk):
        total = keep_ref[chunk].astype(F32) + other_ref[chunk].astype(F32)
        out_ref[chunk] = total.astype(BF16)


def plane_kernel(parts_ref, out_ref):
    def total(rows):
        terms = parts_ref[0, rows].astype(F32)
        for chunk in range(1, 32):
            terms = terms + parts_ref[chunk, rows].astype(F32)
        return terms.astype(BF16)

    gain = total(slice(128, 136))
    for z in range(16):
        out_ref[z, 64:72] = gain

    for zh in range(2):
        tiles = total(slice(zh * 64, zh * 64 + 64))
        for zl in range(8):
            out_ref[zh * 8 + zl, 0:64] = tiles


def column_kernel(parts_ref, half_ref, gain_ref):
    for side in range(2):
        total = parts_ref[side, 0:64].astype(F32)
        for z in range(2 + side, 16, 2):
            total = total + parts_ref[z, 0:64].astype(F32)
        half_ref[side * 64 : side * 64 + 64] = total.astype(BF16)
    gain = parts_ref[0, 64:72].astype(F32)
    for z in range(2, 16, 2):
        gain = gain + parts_ref[z, 64:72].astype(F32)
    gain_ref[...] = gain[0:4] + gain[4:8]


def spread_kernel(place, own_ref, other_ref, qkv_ref, out_ref):
    core = place[2]
    for j in range(16):
        rows = slice(j % 8 * 16, j % 8 * 16 + 16)
        own, other = own_ref[rows].astype(F32), other_ref[rows].astype(F32)
        tile = jnp.where(core == j // 8, own, other)
        if j < 12:
            qkv_ref[:, 128 * j : 128 * (j + 1)] = tile
        else:
            out_ref[:, 128 * (j - 12) : 128 * (j - 11)] = tile


def index(zh, y, x, zl, c):
    return (((zh * 4 + y) * 4 + x) * 8 + zl) * 2 + c


def in_one_piece(work, start):
    once = jnp.minimum(lax.axis_index(LAT) + 1, 1)

    def body(turn, values):
        values, _ = lax.optimization_barrier((values, turn))
        return work(*values)

    return lax.fori_loop(0, once, body, start)


def middle_of(zh, lat):
    zl, c = lat // 2, lat % 2
    y, x = MIDS[zl]
    z = (zh * 8 + zl + 1 - 2 * c) % 16
    return index(z // 8, y, x, z % 8, c)


def fetch(blocks, corner, top, first_block):
    out, out_corner, onward = [], [], []
    for zh in range(2):
        for lat in range(16):
            middle, target = middle_of(zh, lat), index(1 - zh, 3, 3, lat // 2, lat % 2)
            out.append((index(zh, 0, 0, lat // 2, lat % 2), middle))
            onward.append((middle, target))
            if lat < 15:
                out_corner.append((index(zh, 0, 0, (lat + 1) // 2, (lat + 1) % 2), middle))
    halfway = lax.ppermute(blocks, ALL, out)
    halfway_corner = lax.ppermute(corner, ALL, out_corner)
    halfway, halfway_corner, blocks, corner, top, first_block = lax.optimization_barrier(
        (halfway, halfway_corner, blocks, corner, top, first_block)
    )
    crossed = lax.ppermute(jnp.concatenate([halfway, halfway_corner[None]]), ALL, onward)
    inner = [i for i in range(32) if i % 16 < 15]

    def usual(blocks, corner, top, first_block):
        return (
            lax.ppermute(blocks, LON, [(i + 1, i) for i in inner]),
            lax.ppermute(
                corner, ALL, [((i + 1) * 16 + j + 1, i * 16 + j) for i in inner for j in range(15)]
            ),
            lax.ppermute(top, LAT, [(j + 1, j) for j in range(15)]),
            lax.ppermute(first_block, ALL, [((i + 1) % 32 * 16, i * 16) for i in range(32)]),
        )

    usual_blocks = in_one_piece(usual, (blocks, corner, top, first_block))
    normal, normal_corner, lat_block, extra = usual_blocks
    return normal, normal_corner, crossed, lat_block, extra


def per_device(block_input, cotangent, norm_gain, w_qkv, w_out):
    half_lat, half_lon = WLAT // 2, WLON // 2
    levels, lat_rows, lon_cols, feature = block_input.shape
    west, corner, top, own = pack(block_input, cotangent)
    fetched = fetch(west, corner, top, corner)
    lat = lax.axis_index(LAT)
    first = lat == 0
    east = lax.axis_index(LON) % 16 == 15
    place = jnp.stack([first, lat == 15, lax.axis_index("c"), east]).astype(jnp.int32)
    drolled, back, grads, hidden, dqkv, *attended, gain_tile, nothing = block(
        place, own, *fetched, norm_gain.reshape(1, feature), w_qkv, w_out
    )

    back_lon = lax.ppermute(back, LON, [(i, (i + 1) % 32) for i in range(32)])

    def sum_in_planes(*operands):
        keep, send = weight_terms(place, *operands[:-1])
        other = lax.ppermute(send, "c", [(0, 1), (1, 0)])
        pair = small_call(
            pair_kernel, "pair_sum", jax.ShapeDtypeStruct((32, 136, 128), BF16),
            keep.reshape(32, 136, 128), other.reshape(32, 136, 128),
        )
        plane = lax.all_to_all(pair, ("y", "x", "zb"), 0, 0, tiled=True)
        plane = small_call(
            plane_kernel, "plane_sum", jax.ShapeDtypeStruct((16, 72, 128), BF16), plane
        )
        return *operands[:-1], plane

    *_, plane = in_one_piece(
        sum_in_planes, (hidden, dqkv, *attended, grads, gain_tile, nothing)
    )
    plane, back_lon = lax.optimization_barrier((plane, back_lon))
    back_lat = lax.ppermute(
        jnp.stack([drolled[252:288], back_lon[108:144]]), LAT, [(j, j + 1) for j in range(15)]
    )
    column = lax.all_to_all(plane, ALONG_Z, 0, 0, tiled=True)
    def grid(piece):
        return piece.reshape(half_lat, half_lon, levels, feature)

    rows = [
        (jnp.where(first, back_lon[144:180], back_lat[1]), jnp.where(first, drolled[288:324], back_lat[0])),
        (back_lon[0:36], drolled[0:36]),
        (back_lon[36:72], drolled[36:72]),
        (back_lon[72:108], drolled[144:180]),
    ]
    input_grad = jnp.concatenate(
        [jnp.concatenate([grid(west), grid(east)], axis=1) for west, east in rows], axis=0
    )
    column, input_grad = lax.optimization_barrier((column, input_grad))
    half, gain_rows = small_call(
        column_kernel, "column_sum",
        (jax.ShapeDtypeStruct((128, 128), BF16), jax.ShapeDtypeStruct((4, 128), F32)),
        column,
    )
    gain_grad = gain_rows.reshape(feature)
    other_half = lax.ppermute(half, "c", [(0, 1), (1, 0)])
    qkv_grad, out_grad = small_call(
        spread_kernel, "spread",
        (
            jax.ShapeDtypeStruct((16, 3 * feature), F32),
            jax.ShapeDtypeStruct((16, feature), F32),
        ),
        half, other_half, place=place,
    )

    input_grad = input_grad.transpose(2, 0, 1, 3)
    return input_grad, qkv_grad, out_grad, gain_grad


def solution(mesh):
    fine = Mesh(mesh.devices.reshape(2, 4, 4, 4, 2, 2), ALL)
    grid_spec = P(None, LAT, LON, None)
    return jax.shard_map(
        per_device,
        mesh=fine,
        in_specs=(grid_spec, grid_spec, P(), P(), P()),
        out_specs=(grid_spec, P(LON, None), P(LON, None), P()),
        check_vma=False,
    )
```

```python
import functools
import math

import jax
import jax.numpy as jnp
from jax import lax
from jax.experimental import pallas as pl
from jax.experimental.pallas import tpu as pltpu
from jax.sharding import Mesh, PartitionSpec as P

HEADS = 16
HEAD_DIM = 32
WLAT = 6
WLON = 12
WINDOW = 144
TOKENS = 288
HALF = 72
EXTRA = 80
ALL_TOKENS = TOKENS + EXTRA
BLOCK = 36
GROUP = 4
BF16 = jnp.bfloat16
F32 = jnp.float32
LON = ("zh", "y", "x")
LAT = ("zq", "zb", "c")
ALONG_Z = ("zh", "zq", "zb")
ALL = LON + LAT
MIDS = ((0, 3), (3, 0), (3, 1), (1, 3), (2, 0), (0, 2), (1, 0), (2, 3))


def nn(a, b):
    return lax.dot_general(a, b, (((1,), (0,)), ((), ())), preferred_element_type=F32)


def nt(a, b):
    return lax.dot_general(a, b, (((1,), (1,)), ((), ())), preferred_element_type=F32)


def tn(a, b):
    return lax.dot_general(a, b, (((0,), (0,)), ((), ())), preferred_element_type=F32)


def attention_group(start, size, masked, group, qkv, d_attn, attended_t, dqkv):
    feature = HEADS * HEAD_DIM
    width = GROUP * HEAD_DIM
    rows = pl.ds(start, size)
    at = group * width

    def columns(offset):
        return pl.ds(pl.multiple_of(at + offset, 128), width)

    queries = qkv[rows, columns(0)]
    keys = qkv[rows, columns(feature)]
    values = qkv[rows, columns(2 * feature)]
    grads = d_attn[rows, columns(0)]
    scale = 1.0 / math.sqrt(HEAD_DIM)
    lane_head = lax.broadcasted_iota(jnp.int32, (1, width), 1) // HEAD_DIM
    key_late = lax.broadcasted_iota(jnp.int32, (size, size), 0) >= HALF
    query_late = lax.broadcasted_iota(jnp.int32, (size, size), 1) >= HALF
    allowed = jnp.logical_or(key_late == query_late, jnp.logical_not(masked))

    own = [(lane_head == head).astype(BF16) for head in range(GROUP)]
    key_stack = jnp.concatenate([keys * mask for mask in own], axis=0)
    value_stack = jnp.concatenate([values * mask for mask in own], axis=0)
    scores_all = nt(key_stack, queries)
    dprob_all = nt(value_stack, grads)
    prob_parts, dscore_parts = [], []
    for head in range(GROUP):
        part = slice(head * size, (head + 1) * size)
        scores = jnp.where(allowed, scores_all[part] * (scale * math.log2(math.e)), -jnp.inf)
        weights = jnp.exp2(scores - jnp.max(scores, axis=0, keepdims=True))
        prob = weights * (1.0 / jnp.sum(weights, axis=0, keepdims=True))
        dprob = dprob_all[part]
        delta = jnp.sum(prob * dprob, axis=0, keepdims=True)
        dscore_parts.append((prob * (dprob - delta) * scale).astype(BF16))
        prob_parts.append(prob.astype(BF16))
    prob_all = jnp.concatenate(prob_parts, axis=0)
    dscore_all = jnp.concatenate(dscore_parts, axis=0)

    def own_columns(stack):
        picked = stack[0:size]
        for head in range(1, GROUP):
            picked = jnp.where(lane_head == head, stack[head * size : (head + 1) * size], picked)
        return picked.astype(BF16)

    def turned(array):
        return array.astype(F32).T.astype(BF16)

    def by_head(heads_t, parts):
        return jnp.concatenate(
            [
                nn(heads_t[head * HEAD_DIM : (head + 1) * HEAD_DIM], parts[head])
                for head in range(GROUP)
            ],
            axis=0,
        )

    attended_t[pl.ds(pl.multiple_of(at, 128), width), :] = by_head(
        turned(values), prob_parts
    ).astype(BF16)
    dqkv[rows, columns(0)] = by_head(turned(keys), dscore_parts).T.astype(BF16)
    dqkv[rows, columns(feature)] = own_columns(nn(dscore_all, queries))
    dqkv[rows, columns(2 * feature)] = own_columns(nn(prob_all, grads))


def block_kernel(
    place, own_ref, usual_ref, usual_corner_ref, crossed_ref, lat_ref, extra_ref,
    gain_ref, w_qkv_ref, w_out_ref,
    drolled_ref, back_ref, dy_ref, hidden_ref, dqkv_ref, attended_ref, attended_extra_ref,
    gain_tile_ref, nothing_ref,
    x_ref, dy_wide_ref, normed_ref, inverse_ref, qkv_ref, d_attn_ref,
):
    first = place[0]
    last = place[1]
    east = place[3] == 1
    feature = HEADS * HEAD_DIM
    regular = pl.ds(0, TOKENS)
    extra = pl.ds(TOKENS, EXTRA)

    for kind, ref in ((0, x_ref), (1, dy_wide_ref)):

        def fetched(k, usual):
            return jnp.where(east, crossed_ref[k, kind].astype(F32), usual.astype(F32))

        blocks = (
            own_ref[0, kind], own_ref[1, kind], fetched(0, usual_ref[0, kind]),
            fetched(1, usual_ref[1, kind]), own_ref[2, kind], fetched(2, usual_ref[2, kind]),
            fetched(3, usual_corner_ref[kind]), lat_ref[kind], own_ref[3, kind], extra_ref[kind],
        )
        for at, part in enumerate(blocks):
            ref[at * BLOCK : (at + 1) * BLOCK, :] = part.astype(F32)
        ref[TOKENS + HALF :, :] = jnp.zeros((EXTRA - HALF, feature), F32)
    dy_ref[...] = dy_wide_ref[...].astype(BF16)

    def project(rows):
        values = x_ref[rows, :]
        centred = values - jnp.mean(values, axis=-1, keepdims=True)
        inverse = lax.rsqrt(jnp.mean(centred * centred, axis=-1, keepdims=True) + 1e-05)
        normed = centred * inverse
        normed_ref[rows, :] = normed
        inverse_ref[rows, :] = jnp.broadcast_to(inverse, (inverse.shape[0], 128))
        hidden = (normed * gain_ref[...]).astype(BF16)
        hidden_ref[rows, :] = hidden
        qkv_ref[rows, :] = nn(hidden, w_qkv_ref[...]).astype(BF16)
        d_attn_ref[rows, :] = nt(dy_ref[rows, :], w_out_ref[...]).astype(BF16)

    def finish(rows):
        dhidden = nt(dqkv_ref[rows, :], w_qkv_ref[...])
        normed = normed_ref[rows, :]
        dnorm = dhidden * gain_ref[...]
        drolled = dy_wide_ref[rows, :] + inverse_ref[rows, 0:1] * (
            dnorm
            - jnp.mean(dnorm, axis=-1, keepdims=True)
            - normed * jnp.mean(dnorm * normed, axis=-1, keepdims=True)
        )
        drolled_ref[rows, :] = drolled.astype(BF16)
        back_ref[0:72, :] = drolled[72:144].astype(BF16)
        back_ref[72:144, :] = drolled[180:252].astype(BF16)
        if drolled.shape[0] > TOKENS:
            back_ref[144:180, :] = drolled[324:360].astype(BF16)
        else:
            back_ref[144:180, :] = jnp.zeros((BLOCK, feature), BF16)

        gain_local = jnp.sum(dhidden * normed, axis=0, keepdims=True)
        coarse = gain_local.astype(BF16)
        fine = (gain_local - coarse.astype(F32)).astype(BF16)
        parts = [part[:, 128 * j : 128 * (j + 1)] for part in (coarse, fine) for j in range(4)]
        gain_tile_ref[...] = jnp.concatenate(
            [part.astype(F32) for part in parts], axis=0
        ).astype(BF16)

    groups = HEADS // GROUP

    def attention(windows):
        @pl.loop(0, windows * groups, unroll=4)
        def _(step):
            window = step // groups
            attention_group(
                pl.multiple_of(window * WINDOW, 16), WINDOW,
                jnp.logical_and(last == 1, window == 1), step % groups,
                qkv_ref, d_attn_ref, attended_ref.at[window], dqkv_ref,
            )

    @pl.when(first == 0)
    def _():
        project(regular)
        attention(TOKENS // WINDOW)
        finish(regular)
        hidden_ref[extra, :] = jnp.zeros((EXTRA, feature), BF16)
        attended_extra_ref[...] = jnp.zeros((feature, EXTRA), BF16)
        dqkv_ref[extra, :] = jnp.zeros((EXTRA, 3 * feature), BF16)
        drolled_ref[extra, :] = jnp.zeros((EXTRA, feature), BF16)

    @pl.when(first == 1)
    def _():
        project(pl.ds(0, ALL_TOKENS))
        attention(TOKENS // WINDOW)

        @pl.loop(0, groups, unroll=4)
        def _(group):
            attention_group(
                TOKENS, EXTRA, first == 1, group,
                qkv_ref, d_attn_ref, attended_extra_ref, dqkv_ref,
            )

        finish(pl.ds(0, ALL_TOKENS))

    nothing_ref[...] = jnp.zeros(nothing_ref.shape, BF16)


def block(place, *operands):
    feature = HEADS * HEAD_DIM
    vmem = pl.BlockSpec(memory_space=pltpu.VMEM)

    def half(*shape):
        return jax.ShapeDtypeStruct(shape, BF16)

    return pl.pallas_call(
        block_kernel,
        out_shape=(
            half(ALL_TOKENS, feature), half(5 * BLOCK, feature), half(ALL_TOKENS, feature),
            half(ALL_TOKENS, feature), half(ALL_TOKENS, 3 * feature),
            half(TOKENS // WINDOW, feature, WINDOW), half(feature, EXTRA),
            half(8, 128), half(16, 72, 128),
        ),
        in_specs=[pl.BlockSpec(memory_space=pltpu.SMEM)] + [vmem] * len(operands),
        out_specs=(vmem,) * 9,
        scratch_shapes=[
            pltpu.VMEM((ALL_TOKENS, feature), F32),
            pltpu.VMEM((ALL_TOKENS, feature), F32),
            pltpu.VMEM((ALL_TOKENS, feature), F32),
            pltpu.VMEM((ALL_TOKENS, 128), F32),
            pltpu.VMEM((ALL_TOKENS, 3 * feature), BF16),
            pltpu.VMEM((ALL_TOKENS, feature), BF16),
        ],
        compiler_params=pltpu.CompilerParams(vmem_limit_bytes=40 * 1024 * 1024),
        cost_estimate=pl.CostEstimate(
            flops=2_000_000_000, bytes_accessed=6_000_000, transcendentals=700_000
        ),
        name="window_block",
    )(place, *operands)


def weights_kernel(
    place, hidden_ref, dqkv_ref, attended_ref, attended_extra_ref, dy_ref, gain_tile_ref,
    keep_ref, send_ref, total_ref,
):
    core = place[2]
    feature = HEADS * HEAD_DIM
    total_ref[:, 0 : 3 * feature] = tn(hidden_ref[...], dqkv_ref[...]).astype(BF16)
    out_total = nn(attended_extra_ref[...], dy_ref[TOKENS:, :])
    for window in range(TOKENS // WINDOW):
        rows = slice(window * WINDOW, (window + 1) * WINDOW)
        out_total = out_total + nn(attended_ref[window], dy_ref[rows, :])
    total_ref[:, 3 * feature :] = out_total.astype(BF16)
    for lon in range(16):
        for ref in (keep_ref, send_ref):
            ref[lon, 0, 128:136] = gain_tile_ref[...]
            ref[lon, 1, 128:136] = gain_tile_ref[...]

    def deal(halves):
        @pl.loop(0, 16)
        def _(lon):
            for zh in range(2):
                start = pl.multiple_of(zh * 256 + lon * 16, 16)
                rows = total_ref[pl.ds(start, 16), :]
                for j in range(16):
                    tile = (zh * 4 + j % 4) * 16
                    halves[j // 8][lon, j % 8 // 4, tile : tile + 16] = rows[:, 128 * j : 128 * (j + 1)]

    @pl.when(core == 0)
    def _():
        deal((keep_ref, send_ref))

    @pl.when(core == 1)
    def _():
        deal((send_ref, keep_ref))


def weight_terms(place, *operands):
    feature = HEADS * HEAD_DIM
    vmem = pl.BlockSpec(memory_space=pltpu.VMEM)
    dealt = jax.ShapeDtypeStruct((16, 2, 136, 128), BF16)
    return pl.pallas_call(
        weights_kernel,
        out_shape=(dealt, dealt),
        in_specs=[pl.BlockSpec(memory_space=pltpu.SMEM)] + [vmem] * len(operands),
        out_specs=(vmem, vmem),
        scratch_shapes=[pltpu.VMEM((feature, 4 * feature), BF16)],
        compiler_params=pltpu.CompilerParams(vmem_limit_bytes=40 * 1024 * 1024),
        cost_estimate=pl.CostEstimate(
            flops=700_000_000, bytes_accessed=4_000_000, transcendentals=0
        ),
        name="weight_terms",
    )(place, *operands)


def small_call(body, name, out_shape, *operands, place=None):
    vmem = pl.BlockSpec(memory_space=pltpu.VMEM)
    many = isinstance(out_shape, tuple)
    head = () if place is None else (place,)
    return pl.pallas_call(
        body,
        out_shape=out_shape,
        in_specs=[pl.BlockSpec(memory_space=pltpu.SMEM)] * len(head) + [vmem] * len(operands),
        out_specs=(vmem,) * len(out_shape) if many else vmem,
        compiler_params=pltpu.CompilerParams(vmem_limit_bytes=8 * 1024 * 1024),
        name=name,
    )(*head, *operands)


def pack_kernel(x_ref, dy_ref, west_ref, corner_ref, top_ref, own_ref, wide_ref):
    for kind, ref in ((0, x_ref), (1, dy_ref)):
        for band in range(4):
            for side in range(2):
                at = (kind * 4 + band) * 2 + side
                for i in range(BLOCK // 2):
                    pair = ref[band * 3 + i // 6, side * 6 + i % 6]
                    wide_ref[at, 2 * i : 2 * i + 2, :] = pair.astype(F32)
                part = wide_ref[at].astype(BF16)
                if side == 1:
                    own_ref[(band + 3) % 4, kind] = part
                    if band == 0:
                        top_ref[kind] = part
                elif band == 0:
                    corner_ref[kind] = part
                else:
                    west_ref[band - 1, kind] = part


def pack(block_input, cotangent):
    feature = block_input.shape[-1]
    vmem = pl.BlockSpec(memory_space=pltpu.VMEM)

    def blocks(*lead):
        return jax.ShapeDtypeStruct((*lead, 2, BLOCK, feature), BF16)

    return pl.pallas_call(
        pack_kernel,
        out_shape=(blocks(3), blocks(), blocks(), blocks(4)),
        in_specs=[vmem] * 2,
        out_specs=(vmem,) * 4,
        scratch_shapes=[pltpu.VMEM((16, BLOCK, feature), F32)],
        compiler_params=pltpu.CompilerParams(vmem_limit_bytes=16 * 1024 * 1024),
        name="pack",
    )(block_input.transpose(1, 2, 0, 3), cotangent.transpose(1, 2, 0, 3))


def pair_kernel(keep_ref, other_ref, out_ref):
    @pl.loop(0, 32)
    def _(chunk):
        total = keep_ref[chunk].astype(F32) + other_ref[chunk].astype(F32)
        out_ref[chunk] = total.astype(BF16)


def plane_kernel(parts_ref, out_ref):
    def total(rows):
        terms = parts_ref[0, rows].astype(F32)
        for chunk in range(1, 32):
            terms = terms + parts_ref[chunk, rows].astype(F32)
        return terms.astype(BF16)

    gain = total(slice(128, 136))
    for z in range(16):
        out_ref[z, 64:72] = gain

    for zh in range(2):
        tiles = total(slice(zh * 64, zh * 64 + 64))
        for zl in range(8):
            out_ref[zh * 8 + zl, 0:64] = tiles


def column_kernel(parts_ref, half_ref, gain_ref):
    for side in range(2):
        total = parts_ref[side, 0:64].astype(F32)
        for z in range(2 + side, 16, 2):
            total = total + parts_ref[z, 0:64].astype(F32)
        half_ref[side * 64 : side * 64 + 64] = total.astype(BF16)
    gain = parts_ref[0, 64:72].astype(F32)
    for z in range(2, 16, 2):
        gain = gain + parts_ref[z, 64:72].astype(F32)
    gain_ref[...] = gain[0:4] + gain[4:8]


def spread_kernel(place, own_ref, other_ref, qkv_ref, out_ref):
    core = place[2]
    for j in range(16):
        rows = slice(j % 8 * 16, j % 8 * 16 + 16)
        own, other = own_ref[rows].astype(F32), other_ref[rows].astype(F32)
        tile = jnp.where(core == j // 8, own, other)
        if j < 12:
            qkv_ref[:, 128 * j : 128 * (j + 1)] = tile
        else:
            out_ref[:, 128 * (j - 12) : 128 * (j - 11)] = tile


def index(zh, y, x, zl, c):
    return (((zh * 4 + y) * 4 + x) * 8 + zl) * 2 + c


def in_one_piece(work, start):
    once = jnp.minimum(lax.axis_index(LAT) + 1, 1)

    def body(turn, values):
        values, _ = lax.optimization_barrier((values, turn))
        return work(*values)

    return lax.fori_loop(0, once, body, start)


def middle_of(zh, lat):
    zl, c = lat // 2, lat % 2
    y, x = MIDS[zl]
    z = (zh * 8 + zl + 1 - 2 * c) % 16
    return index(z // 8, y, x, z % 8, c)


def fetch(blocks, corner, top, first_block):
    out, out_corner, onward = [], [], []
    for zh in range(2):
        for lat in range(16):
            middle, target = middle_of(zh, lat), index(1 - zh, 3, 3, lat // 2, lat % 2)
            out.append((index(zh, 0, 0, lat // 2, lat % 2), middle))
            onward.append((middle, target))
            if lat < 15:
                out_corner.append((index(zh, 0, 0, (lat + 1) // 2, (lat + 1) % 2), middle))
    halfway = lax.ppermute(blocks, ALL, out)
    halfway_corner = lax.ppermute(corner, ALL, out_corner)
    halfway, halfway_corner, blocks, corner, top, first_block = lax.optimization_barrier(
        (halfway, halfway_corner, blocks, corner, top, first_block)
    )
    crossed = lax.ppermute(jnp.concatenate([halfway, halfway_corner[None]]), ALL, onward)
    inner = [i for i in range(32) if i % 16 < 15]

    def usual(blocks, corner, top, first_block):
        return (
            lax.ppermute(blocks, LON, [(i + 1, i) for i in inner]),
            lax.ppermute(
                corner, ALL, [((i + 1) * 16 + j + 1, i * 16 + j) for i in inner for j in range(15)]
            ),
            lax.ppermute(top, LAT, [(j + 1, j) for j in range(15)]),
            lax.ppermute(first_block, ALL, [((i + 1) % 32 * 16, i * 16) for i in range(32)]),
        )

    usual_blocks = in_one_piece(usual, (blocks, corner, top, first_block))
    normal, normal_corner, lat_block, extra = usual_blocks
    return normal, normal_corner, crossed, lat_block, extra


def per_device(block_input, cotangent, norm_gain, w_qkv, w_out):
    half_lat, half_lon = WLAT // 2, WLON // 2
    levels, lat_rows, lon_cols, feature = block_input.shape
    west, corner, top, own = pack(block_input, cotangent)
    fetched = fetch(west, corner, top, corner)
    lat = lax.axis_index(LAT)
    first = lat == 0
    east = lax.axis_index(LON) % 16 == 15
    place = jnp.stack([first, lat == 15, lax.axis_index("c"), east]).astype(jnp.int32)
    drolled, back, grads, hidden, dqkv, *attended, gain_tile, nothing = block(
        place, own, *fetched, norm_gain.reshape(1, feature), w_qkv, w_out
    )

    back_lon = lax.ppermute(back, LON, [(i, (i + 1) % 32) for i in range(32)])

    def sum_in_planes(*operands):
        keep, send = weight_terms(place, *operands[:-1])
        other = lax.ppermute(send, "c", [(0, 1), (1, 0)])
        pair = small_call(
            pair_kernel, "pair_sum", jax.ShapeDtypeStruct((32, 136, 128), BF16),
            keep.reshape(32, 136, 128), other.reshape(32, 136, 128),
        )
        plane = lax.all_to_all(pair, ("y", "x", "zb"), 0, 0, tiled=True)
        plane = small_call(
            plane_kernel, "plane_sum", jax.ShapeDtypeStruct((16, 72, 128), BF16), plane
        )
        return *operands[:-1], plane

    *_, plane = in_one_piece(
        sum_in_planes, (hidden, dqkv, *attended, grads, gain_tile, nothing)
    )
    plane, back_lon = lax.optimization_barrier((plane, back_lon))
    back_lat = lax.ppermute(
        jnp.stack([drolled[252:288], back_lon[108:144]]), LAT, [(j, j + 1) for j in range(15)]
    )
    column = lax.all_to_all(plane, ALONG_Z, 0, 0, tiled=True)
    def grid(piece):
        return piece.reshape(half_lat, half_lon, levels, feature)

    rows = [
        (jnp.where(first, back_lon[144:180], back_lat[1]), jnp.where(first, drolled[288:324], back_lat[0])),
        (back_lon[0:36], drolled[0:36]),
        (back_lon[36:72], drolled[36:72]),
        (back_lon[72:108], drolled[144:180]),
    ]
    input_grad = jnp.concatenate(
        [jnp.concatenate([grid(west), grid(east)], axis=1) for west, east in rows], axis=0
    )
    column, input_grad = lax.optimization_barrier((column, input_grad))
    half, gain_rows = small_call(
        column_kernel, "column_sum",
        (jax.ShapeDtypeStruct((128, 128), BF16), jax.ShapeDtypeStruct((4, 128), F32)),
        column,
    )
    gain_grad = gain_rows.reshape(feature)
    other_half = lax.ppermute(half, "c", [(0, 1), (1, 0)])
    qkv_grad, out_grad = small_call(
        spread_kernel, "spread",
        (
            jax.ShapeDtypeStruct((16, 3 * feature), F32),
            jax.ShapeDtypeStruct((16, feature), F32),
        ),
        half, other_half, place=place,
    )

    input_grad = input_grad.transpose(2, 0, 1, 3)
    return input_grad, qkv_grad, out_grad, gain_grad


def solution(mesh):
    fine = Mesh(mesh.devices.reshape(2, 4, 4, 4, 2, 2), ALL)
    grid_spec = P(None, LAT, LON, None)
    return jax.shard_map(
        per_device,
        mesh=fine,
        in_specs=(grid_spec, grid_spec, P(), P(), P()),
        out_specs=(grid_spec, P(LON, None), P(LON, None), P()),
        check_vma=False,
    )
```

```python
import functools
import math

import jax
import jax.numpy as jnp
from jax import lax
from jax.experimental import pallas as pl
from jax.experimental.pallas import tpu as pltpu
from jax.sharding import Mesh, PartitionSpec as P

HEADS = 16
HEAD_DIM = 32
WLAT = 6
WLON = 12
WINDOW = 144
TOKENS = 288
HALF = 72
EXTRA = 80
ALL_TOKENS = TOKENS + EXTRA
BLOCK = 36
GROUP = 4
BF16 = jnp.bfloat16
F32 = jnp.float32
LON = ("zh", "y", "x")
LAT = ("zq", "zb", "c")
ALONG_Z = ("zh", "zq", "zb")
ALL = LON + LAT
MIDS = ((0, 3), (3, 0), (3, 1), (1, 3), (2, 0), (0, 2), (1, 0), (2, 3))


def nn(a, b):
    return lax.dot_general(a, b, (((1,), (0,)), ((), ())), preferred_element_type=F32)


def nt(a, b):
    return lax.dot_general(a, b, (((1,), (1,)), ((), ())), preferred_element_type=F32)


def tn(a, b):
    return lax.dot_general(a, b, (((0,), (0,)), ((), ())), preferred_element_type=F32)


def attention_group(start, size, masked, group, qkv, d_attn, attended_t, dqkv):
    feature = HEADS * HEAD_DIM
    width = GROUP * HEAD_DIM
    rows = pl.ds(start, size)
    at = group * width

    def columns(offset):
        return pl.ds(pl.multiple_of(at + offset, 128), width)

    queries = qkv[rows, columns(0)]
    keys = qkv[rows, columns(feature)]
    values = qkv[rows, columns(2 * feature)]
    grads = d_attn[rows, columns(0)]
    scale = 1.0 / math.sqrt(HEAD_DIM)
    lane_head = lax.broadcasted_iota(jnp.int32, (1, width), 1) // HEAD_DIM
    key_late = lax.broadcasted_iota(jnp.int32, (size, size), 0) >= HALF
    query_late = lax.broadcasted_iota(jnp.int32, (size, size), 1) >= HALF
    allowed = jnp.logical_or(key_late == query_late, jnp.logical_not(masked))

    own = [(lane_head == head).astype(BF16) for head in range(GROUP)]
    key_stack = jnp.concatenate([keys * mask for mask in own], axis=0)
    value_stack = jnp.concatenate([values * mask for mask in own], axis=0)
    scores_all = nt(key_stack, queries)
    dprob_all = nt(value_stack, grads)
    prob_parts, dscore_parts = [], []
    for head in range(GROUP):
        part = slice(head * size, (head + 1) * size)
        scores = jnp.where(allowed, scores_all[part] * (scale * math.log2(math.e)), -jnp.inf)
        weights = jnp.exp2(scores - jnp.max(scores, axis=0, keepdims=True))
        prob = weights * (1.0 / jnp.sum(weights, axis=0, keepdims=True))
        dprob = dprob_all[part]
        delta = jnp.sum(prob * dprob, axis=0, keepdims=True)
        dscore_parts.append((prob * (dprob - delta) * scale).astype(BF16))
        prob_parts.append(prob.astype(BF16))
    prob_all = jnp.concatenate(prob_parts, axis=0)
    dscore_all = jnp.concatenate(dscore_parts, axis=0)

    def own_columns(stack):
        picked = stack[0:size]
        for head in range(1, GROUP):
            picked = jnp.where(lane_head == head, stack[head * size : (head + 1) * size], picked)
        return picked.astype(BF16)

    def turned(array):
        return array.astype(F32).T.astype(BF16)

    def by_head(heads_t, parts):
        return jnp.concatenate(
            [
                nn(heads_t[head * HEAD_DIM : (head + 1) * HEAD_DIM], parts[head])
                for head in range(GROUP)
            ],
            axis=0,
        )

    attended_t[pl.ds(pl.multiple_of(at, 128), width), :] = by_head(
        turned(values), prob_parts
    ).astype(BF16)
    dqkv[rows, columns(0)] = by_head(turned(keys), dscore_parts).T.astype(BF16)
    dqkv[rows, columns(feature)] = own_columns(nn(dscore_all, queries))
    dqkv[rows, columns(2 * feature)] = own_columns(nn(prob_all, grads))


def block_kernel(
    place, own_ref, usual_ref, usual_corner_ref, crossed_ref, lat_ref, extra_ref,
    gain_ref, w_qkv_ref, w_out_ref,
    drolled_ref, back_ref, dy_ref, hidden_ref, dqkv_ref, attended_ref, attended_extra_ref,
    gain_tile_ref, nothing_ref,
    x_ref, dy_wide_ref, normed_ref, inverse_ref, qkv_ref, d_attn_ref,
):
    first = place[0]
    last = place[1]
    east = place[3] == 1
    feature = HEADS * HEAD_DIM
    regular = pl.ds(0, TOKENS)
    extra = pl.ds(TOKENS, EXTRA)

    for kind, ref in ((0, x_ref), (1, dy_wide_ref)):

        def fetched(k, usual):
            return jnp.where(east, crossed_ref[k, kind].astype(F32), usual.astype(F32))

        blocks = (
            own_ref[0, kind], own_ref[1, kind], fetched(0, usual_ref[0, kind]),
            fetched(1, usual_ref[1, kind]), own_ref[2, kind], fetched(2, usual_ref[2, kind]),
            fetched(3, usual_corner_ref[kind]), lat_ref[kind], own_ref[3, kind], extra_ref[kind],
        )
        for at, part in enumerate(blocks):
            ref[at * BLOCK : (at + 1) * BLOCK, :] = part.astype(F32)
        ref[TOKENS + HALF :, :] = jnp.zeros((EXTRA - HALF, feature), F32)
    dy_ref[...] = dy_wide_ref[...].astype(BF16)

    def project(rows):
        values = x_ref[rows, :]
        centred = values - jnp.mean(values, axis=-1, keepdims=True)
        inverse = lax.rsqrt(jnp.mean(centred * centred, axis=-1, keepdims=True) + 1e-05)
        normed = centred * inverse
        normed_ref[rows, :] = normed
        inverse_ref[rows, :] = jnp.broadcast_to(inverse, (inverse.shape[0], 128))
        hidden = (normed * gain_ref[...]).astype(BF16)
        hidden_ref[rows, :] = hidden
        qkv_ref[rows, :] = nn(hidden, w_qkv_ref[...]).astype(BF16)
        d_attn_ref[rows, :] = nt(dy_ref[rows, :], w_out_ref[...]).astype(BF16)

    def finish(rows):
        dhidden = nt(dqkv_ref[rows, :], w_qkv_ref[...])
        normed = normed_ref[rows, :]
        dnorm = dhidden * gain_ref[...]
        drolled = dy_wide_ref[rows, :] + inverse_ref[rows, 0:1] * (
            dnorm
            - jnp.mean(dnorm, axis=-1, keepdims=True)
            - normed * jnp.mean(dnorm * normed, axis=-1, keepdims=True)
        )
        drolled_ref[rows, :] = drolled.astype(BF16)
        back_ref[0:72, :] = drolled[72:144].astype(BF16)
        back_ref[72:144, :] = drolled[180:252].astype(BF16)
        if drolled.shape[0] > TOKENS:
            back_ref[144:180, :] = drolled[324:360].astype(BF16)
        else:
            back_ref[144:180, :] = jnp.zeros((BLOCK, feature), BF16)

        gain_local = jnp.sum(dhidden * normed, axis=0, keepdims=True)
        coarse = gain_local.astype(BF16)
        fine = (gain_local - coarse.astype(F32)).astype(BF16)
        parts = [part[:, 128 * j : 128 * (j + 1)] for part in (coarse, fine) for j in range(4)]
        gain_tile_ref[...] = jnp.concatenate(
            [part.astype(F32) for part in parts], axis=0
        ).astype(BF16)

    groups = HEADS // GROUP

    def attention(windows):
        @pl.loop(0, windows * groups, unroll=8)
        def _(step):
            window = step // groups
            attention_group(
                pl.multiple_of(window * WINDOW, 16), WINDOW,
                jnp.logical_and(last == 1, window == 1), step % groups,
                qkv_ref, d_attn_ref, attended_ref.at[window], dqkv_ref,
            )

    @pl.when(first == 0)
    def _():
        project(regular)
        attention(TOKENS // WINDOW)
        finish(regular)
        hidden_ref[extra, :] = jnp.zeros((EXTRA, feature), BF16)
        attended_extra_ref[...] = jnp.zeros((feature, EXTRA), BF16)
        dqkv_ref[extra, :] = jnp.zeros((EXTRA, 3 * feature), BF16)
        drolled_ref[extra, :] = jnp.zeros((EXTRA, feature), BF16)

    @pl.when(first == 1)
    def _():
        project(pl.ds(0, ALL_TOKENS))
        attention(TOKENS // WINDOW)

        @pl.loop(0, groups, unroll=4)
        def _(group):
            attention_group(
                TOKENS, EXTRA, first == 1, group,
                qkv_ref, d_attn_ref, attended_extra_ref, dqkv_ref,
            )

        finish(pl.ds(0, ALL_TOKENS))

    nothing_ref[...] = jnp.zeros(nothing_ref.shape, BF16)


def block(place, *operands):
    feature = HEADS * HEAD_DIM
    vmem = pl.BlockSpec(memory_space=pltpu.VMEM)

    def half(*shape):
        return jax.ShapeDtypeStruct(shape, BF16)

    return pl.pallas_call(
        block_kernel,
        out_shape=(
            half(ALL_TOKENS, feature), half(5 * BLOCK, feature), half(ALL_TOKENS, feature),
            half(ALL_TOKENS, feature), half(ALL_TOKENS, 3 * feature),
            half(TOKENS // WINDOW, feature, WINDOW), half(feature, EXTRA),
            half(8, 128), half(16, 72, 128),
        ),
        in_specs=[pl.BlockSpec(memory_space=pltpu.SMEM)] + [vmem] * len(operands),
        out_specs=(vmem,) * 9,
        scratch_shapes=[
            pltpu.VMEM((ALL_TOKENS, feature), F32),
            pltpu.VMEM((ALL_TOKENS, feature), F32),
            pltpu.VMEM((ALL_TOKENS, feature), F32),
            pltpu.VMEM((ALL_TOKENS, 128), F32),
            pltpu.VMEM((ALL_TOKENS, 3 * feature), BF16),
            pltpu.VMEM((ALL_TOKENS, feature), BF16),
        ],
        compiler_params=pltpu.CompilerParams(vmem_limit_bytes=40 * 1024 * 1024),
        cost_estimate=pl.CostEstimate(
            flops=2_000_000_000, bytes_accessed=6_000_000, transcendentals=700_000
        ),
        name="window_block",
    )(place, *operands)


def weights_kernel(
    kept, place, hidden_ref, dqkv_ref, attended_ref, attended_extra_ref, dy_ref, gain_tile_ref,
    dealt_ref, total_ref,
):
    feature = HEADS * HEAD_DIM
    half = place[2] if kept else 1 - place[2]

    @pl.when(half == 0)
    def _():
        total_ref[...] = tn(hidden_ref[...], dqkv_ref[:, 0 : 2 * feature]).astype(BF16)

    @pl.when(half == 1)
    def _():
        total_ref[:, 0:feature] = tn(hidden_ref[...], dqkv_ref[:, 2 * feature :]).astype(BF16)
        out_total = nn(attended_extra_ref[...], dy_ref[TOKENS:, :])
        for window in range(TOKENS // WINDOW):
            rows = slice(window * WINDOW, (window + 1) * WINDOW)
            out_total = out_total + nn(attended_ref[window], dy_ref[rows, :])
        total_ref[:, feature:] = out_total.astype(BF16)

    for lon in range(16):
        dealt_ref[lon, 0, 128:136] = gain_tile_ref[...]
        dealt_ref[lon, 1, 128:136] = gain_tile_ref[...]

    @pl.loop(0, 16)
    def _(lon):
        for zh in range(2):
            start = pl.multiple_of(zh * 256 + lon * 16, 16)
            rows = total_ref[pl.ds(start, 16), :]
            for j in range(8):
                tile = (zh * 4 + j % 4) * 16
                dealt_ref[lon, j // 4, tile : tile + 16] = rows[:, 128 * j : 128 * (j + 1)]


def weight_terms(kept, place, *operands):
    feature = HEADS * HEAD_DIM
    vmem = pl.BlockSpec(memory_space=pltpu.VMEM)
    return pl.pallas_call(
        functools.partial(weights_kernel, kept),
        out_shape=jax.ShapeDtypeStruct((16, 2, 136, 128), BF16),
        in_specs=[pl.BlockSpec(memory_space=pltpu.SMEM)] + [vmem] * len(operands),
        out_specs=vmem,
        scratch_shapes=[pltpu.VMEM((feature, 2 * feature), BF16)],
        compiler_params=pltpu.CompilerParams(vmem_limit_bytes=40 * 1024 * 1024),
        cost_estimate=pl.CostEstimate(
            flops=2_000_000_000, bytes_accessed=8_000_000, transcendentals=0
        ),
        name="kept_terms" if kept else "sent_terms",
    )(place, *operands)


def small_call(body, name, out_shape, *operands, place=None):
    vmem = pl.BlockSpec(memory_space=pltpu.VMEM)
    many = isinstance(out_shape, tuple)
    head = () if place is None else (place,)
    return pl.pallas_call(
        body,
        out_shape=out_shape,
        in_specs=[pl.BlockSpec(memory_space=pltpu.SMEM)] * len(head) + [vmem] * len(operands),
        out_specs=(vmem,) * len(out_shape) if many else vmem,
        compiler_params=pltpu.CompilerParams(vmem_limit_bytes=8 * 1024 * 1024),
        name=name,
    )(*head, *operands)


def pack_kernel(x_ref, dy_ref, west_ref, corner_ref, top_ref, own_ref, wide_ref):
    for kind, ref in ((0, x_ref), (1, dy_ref)):
        for band in range(4):
            for side in range(2):
                at = (kind * 4 + band) * 2 + side
                for i in range(BLOCK // 2):
                    pair = ref[band * 3 + i // 6, side * 6 + i % 6]
                    wide_ref[at, 2 * i : 2 * i + 2, :] = pair.astype(F32)
                part = wide_ref[at].astype(BF16)
                if side == 1:
                    own_ref[(band + 3) % 4, kind] = part
                    if band == 0:
                        top_ref[kind] = part
                elif band == 0:
                    corner_ref[kind] = part
                else:
                    west_ref[band - 1, kind] = part


def pack(block_input, cotangent):
    feature = block_input.shape[-1]
    vmem = pl.BlockSpec(memory_space=pltpu.VMEM)

    def blocks(*lead):
        return jax.ShapeDtypeStruct((*lead, 2, BLOCK, feature), BF16)

    return pl.pallas_call(
        pack_kernel,
        out_shape=(blocks(3), blocks(), blocks(), blocks(4)),
        in_specs=[vmem] * 2,
        out_specs=(vmem,) * 4,
        scratch_shapes=[pltpu.VMEM((16, BLOCK, feature), F32)],
        compiler_params=pltpu.CompilerParams(vmem_limit_bytes=16 * 1024 * 1024),
        name="pack",
    )(block_input.transpose(1, 2, 0, 3), cotangent.transpose(1, 2, 0, 3))


def pair_kernel(keep_ref, other_ref, out_ref):
    @pl.loop(0, 32)
    def _(chunk):
        total = keep_ref[chunk].astype(F32) + other_ref[chunk].astype(F32)
        out_ref[chunk] = total.astype(BF16)


def plane_kernel(parts_ref, out_ref):
    def total(rows):
        terms = parts_ref[0, rows].astype(F32)
        for chunk in range(1, 32):
            terms = terms + parts_ref[chunk, rows].astype(F32)
        return terms.astype(BF16)

    gain = total(slice(128, 136))
    for z in range(16):
        out_ref[z, 64:72] = gain

    for zh in range(2):
        tiles = total(slice(zh * 64, zh * 64 + 64))
        for zl in range(8):
            out_ref[zh * 8 + zl, 0:64] = tiles


def column_kernel(parts_ref, half_ref, gain_ref):
    for side in range(2):
        total = parts_ref[side, 0:64].astype(F32)
        for z in range(2 + side, 16, 2):
            total = total + parts_ref[z, 0:64].astype(F32)
        half_ref[side * 64 : side * 64 + 64] = total.astype(BF16)
    gain = parts_ref[0, 64:72].astype(F32)
    for z in range(2, 16, 2):
        gain = gain + parts_ref[z, 64:72].astype(F32)
    gain_ref[...] = gain[0:4] + gain[4:8]


def spread_kernel(place, own_ref, other_ref, qkv_ref, out_ref):
    core = place[2]
    for j in range(16):
        rows = slice(j % 8 * 16, j % 8 * 16 + 16)
        own, other = own_ref[rows].astype(F32), other_ref[rows].astype(F32)
        tile = jnp.where(core == j // 8, own, other)
        if j < 12:
            qkv_ref[:, 128 * j : 128 * (j + 1)] = tile
        else:
            out_ref[:, 128 * (j - 12) : 128 * (j - 11)] = tile


def index(zh, y, x, zl, c):
    return (((zh * 4 + y) * 4 + x) * 8 + zl) * 2 + c


def in_one_piece(work, start):
    once = jnp.minimum(lax.axis_index(LAT) + 1, 1)

    def body(turn, values):
        values, _ = lax.optimization_barrier((values, turn))
        return work(*values)

    return lax.fori_loop(0, once, body, start)


def middle_of(zh, lat):
    zl, c = lat // 2, lat % 2
    y, x = MIDS[zl]
    z = (zh * 8 + zl + 1 - 2 * c) % 16
    return index(z // 8, y, x, z % 8, c)


def fetch(blocks, corner, top, first_block):
    out, out_corner, onward = [], [], []
    for zh in range(2):
        for lat in range(16):
            middle, target = middle_of(zh, lat), index(1 - zh, 3, 3, lat // 2, lat % 2)
            out.append((index(zh, 0, 0, lat // 2, lat % 2), middle))
            onward.append((middle, target))
            if lat < 15:
                out_corner.append((index(zh, 0, 0, (lat + 1) // 2, (lat + 1) % 2), middle))
    halfway = lax.ppermute(blocks, ALL, out)
    halfway_corner = lax.ppermute(corner, ALL, out_corner)
    halfway, halfway_corner, blocks, corner, top, first_block = lax.optimization_barrier(
        (halfway, halfway_corner, blocks, corner, top, first_block)
    )
    crossed = lax.ppermute(jnp.concatenate([halfway, halfway_corner[None]]), ALL, onward)
    inner = [i for i in range(32) if i % 16 < 15]

    def usual(blocks, corner, top, first_block):
        return (
            lax.ppermute(blocks, LON, [(i + 1, i) for i in inner]),
            lax.ppermute(
                corner, ALL, [((i + 1) * 16 + j + 1, i * 16 + j) for i in inner for j in range(15)]
            ),
            lax.ppermute(top, LAT, [(j + 1, j) for j in range(15)]),
            lax.ppermute(first_block, ALL, [((i + 1) % 32 * 16, i * 16) for i in range(32)]),
        )

    usual_blocks = in_one_piece(usual, (blocks, corner, top, first_block))
    normal, normal_corner, lat_block, extra = usual_blocks
    return normal, normal_corner, crossed, lat_block, extra


def per_device(block_input, cotangent, norm_gain, w_qkv, w_out):
    half_lat, half_lon = WLAT // 2, WLON // 2
    levels, lat_rows, lon_cols, feature = block_input.shape
    west, corner, top, own = pack(block_input, cotangent)
    fetched = fetch(west, corner, top, corner)
    lat = lax.axis_index(LAT)
    first = lat == 0
    east = lax.axis_index(LON) % 16 == 15
    place = jnp.stack([first, lat == 15, lax.axis_index("c"), east]).astype(jnp.int32)
    drolled, back, grads, hidden, dqkv, *attended, gain_tile, nothing = block(
        place, own, *fetched, norm_gain.reshape(1, feature), w_qkv, w_out
    )

    back_lon = lax.ppermute(back, LON, [(i, (i + 1) % 32) for i in range(32)])

    def sum_in_planes(*operands):
        send = weight_terms(False, place, *operands[:-1])
        other = lax.ppermute(send, "c", [(0, 1), (1, 0)])
        keep = weight_terms(True, place, *operands[:-1])
        pair = small_call(
            pair_kernel, "pair_sum", jax.ShapeDtypeStruct((32, 136, 128), BF16),
            keep.reshape(32, 136, 128), other.reshape(32, 136, 128),
        )
        plane = lax.all_to_all(pair, ("y", "x", "zb"), 0, 0, tiled=True)
        plane = small_call(
            plane_kernel, "plane_sum", jax.ShapeDtypeStruct((16, 72, 128), BF16), plane
        )
        return *operands[:-1], plane

    *_, plane = in_one_piece(
        sum_in_planes, (hidden, dqkv, *attended, grads, gain_tile, nothing)
    )
    plane, back_lon = lax.optimization_barrier((plane, back_lon))
    back_lat = lax.ppermute(
        jnp.stack([drolled[252:288], back_lon[108:144]]), LAT, [(j, j + 1) for j in range(15)]
    )
    column = lax.all_to_all(plane, ALONG_Z, 0, 0, tiled=True)
    def grid(piece):
        return piece.reshape(half_lat, half_lon, levels, feature)

    rows = [
        (jnp.where(first, back_lon[144:180], back_lat[1]), jnp.where(first, drolled[288:324], back_lat[0])),
        (back_lon[0:36], drolled[0:36]),
        (back_lon[36:72], drolled[36:72]),
        (back_lon[72:108], drolled[144:180]),
    ]
    input_grad = jnp.concatenate(
        [jnp.concatenate([grid(west), grid(east)], axis=1) for west, east in rows], axis=0
    )
    column, input_grad = lax.optimization_barrier((column, input_grad))
    half, gain_rows = small_call(
        column_kernel, "column_sum",
        (jax.ShapeDtypeStruct((128, 128), BF16), jax.ShapeDtypeStruct((4, 128), F32)),
        column,
    )
    gain_grad = gain_rows.reshape(feature)
    other_half = lax.ppermute(half, "c", [(0, 1), (1, 0)])
    qkv_grad, out_grad = small_call(
        spread_kernel, "spread",
        (
            jax.ShapeDtypeStruct((16, 3 * feature), F32),
            jax.ShapeDtypeStruct((16, feature), F32),
        ),
        half, other_half, place=place,
    )

    input_grad = input_grad.transpose(2, 0, 1, 3)
    return input_grad, qkv_grad, out_grad, gain_grad


def solution(mesh):
    fine = Mesh(mesh.devices.reshape(2, 4, 4, 4, 2, 2), ALL)
    grid_spec = P(None, LAT, LON, None)
    return jax.shard_map(
        per_device,
        mesh=fine,
        in_specs=(grid_spec, grid_spec, P(), P(), P()),
        out_specs=(grid_spec, P(LON, None), P(LON, None), P()),
        check_vma=False,
    )
```
